32 devices in a mesh: pairs: 2 (over x), rows: 16 (over z, y, core).
Axes of the slice: x: 2, y: 2, z: 4, core: 2. Of those that a mesh axis runs over, the one named last changes fastest.
Arguments:
- frames: bfloat16 [2, 512, 3072], P(None, ('pairs', 'rows')), parts along dimension 1, may hold values from -6 to 6
- conv_weight: bfloat16 [864, 128], replicated, may hold values from -0.21875 to 0.21875
- conv_bias: float32 [128], replicated, may hold values from -3 to 3
- proj_weight: bfloat16 [128, 256], replicated, may hold values from -0.5 to 0.5
- target_row: int32 [12, 4096], P(None, ('pairs', 'rows')), parts along dimension 1, may hold values from 0 to 127
- target_col: int32 [12, 4096], P(None, ('pairs', 'rows')), parts along dimension 1, may hold values from 0 to 15
- cotangent: bfloat16 [3888, 4096], P(None, ('pairs', 'rows')), parts along dimension 1, may hold values from -1.5 to 1.5
Outputs:
- lookups: bfloat16 [3888, 4096], P(None, ('pairs', 'rows')), parts along dimension 1
- grad_input: bfloat16 [2, 512, 3072], P(None, ('pairs', 'rows')), parts along dimension 1
- grad_conv: float32 [1728, 128], P('pairs'), parts along dimension 0
- grad_bias: float32 [256], P('pairs'), parts along dimension 0
- grad_proj: float32 [256, 256], P('pairs'), parts along dimension 0
The draws below stay inside these ranges and needn't reach their ends.
There are 2 independent parts, one for each index of `pairs`. The reference program is written for one: setup_inputs(seed, part) draws one part's arguments, and reference() takes and returns one part's arrays. A program takes and returns all parts, laid end to end along the dimension named above; an argument that names none is the same for every part. Nothing has to cross between parts.
Inputs may be any that keep to these rules, and one draw needn't show every extreme that they name: `target_row`: row of a cell of the feature grid. `target_col`: column of a cell of the feature grid.
All inputs are finite; a program needn't handle non-finite values.
Results may differ from the reference program's by a relative error of at most 0.018.
Values may be sent and summed in bfloat16 or wider, within the bound.
No kernel may reach another device: no remote copies, remote signals or barrier semaphores. Data moves between devices by JAX's collectives and lax.ppermute only.
A program may use at most 128 MiB of HBM per device.

```python
import math
import jax
import jax.numpy as jnp
from jax import lax

C = 256
C1 = 128
C0 = 96
LEVELS = 4
RADIUS = 4
ITERS = 12
RD = 8
WC = 16
NY = 128
PIX = 2048
PACK = 170
LOOKS = 3888
N_ROWS = 16


def touch_ends(values, own_key, smallest, largest):
    extent = values.shape
    place = [jax.random.randint(jax.random.fold_in(own_key, axis), (), 0, extent[axis]) for axis in range(len(extent))]
    values = values.at[tuple(place)].set(smallest)
    longest = extent.index(max(extent))
    place[longest] = (place[longest] + 1) % extent[longest]
    return values.at[tuple(place)].set(largest)


def steps_of(rng, dims, cuts, low, largest):
    factor_of, own = 1.0, jax.random.fold_in(rng, 6)
    for dim, parts in cuts:
        steps = jnp.exp(jax.random.uniform(jax.random.fold_in(own, dim), (parts,), jnp.float32, low / len(cuts), largest / len(cuts)))
        factor_of = factor_of * jnp.repeat(steps, dims[dim] // parts).reshape([-1 if axis == dim else 1 for axis in range(len(dims))])
    return factor_of


def bell_draw(stream_key, shape, deviation, bound, pieces=(), kind=jnp.bfloat16):
    values = deviation * jax.random.normal(stream_key, shape, jnp.float32)
    if pieces:
        values = values * steps_of(stream_key, shape, pieces, -0.22, 0.18)
    return jnp.clip(values, -bound, bound).astype(kind)


def setup_inputs(seed: int = 0, part: int = 0) -> dict:
    streams_of = jax.random.split(jax.random.key(seed), 8)
    part_keys = jax.random.split(jax.random.fold_in(streams_of[7], part), 8)
    return {
        "frames": bell_draw(part_keys[0], (2, 2 * NY, 2 * WC * C0), 1.0, 6.0, ((1, 16),)),
        "conv_weight": bell_draw(streams_of[1], (9 * C0, C1), (9 * C0) ** -0.5, 0.21875),
        "conv_bias": bell_draw(streams_of[2], (C1,), 0.5, 3.0, (), jnp.float32),
        "proj_weight": bell_draw(streams_of[3], (C1, C), C1 ** -0.5, 0.5),
        "target_row": touch_ends(jax.random.randint(part_keys[4], (ITERS, PIX), 0, NY), jax.random.fold_in(part_keys[4], 1), 0, NY - 1).astype(jnp.int32),
        "target_col": touch_ends(jax.random.randint(part_keys[5], (ITERS, PIX), 0, WC), jax.random.fold_in(part_keys[5], 1), 0, WC - 1).astype(jnp.int32),
        "cotangent": bell_draw(part_keys[6], (LOOKS, PIX), 0.25, 1.5, ((1, 16),)),
    }


def window_index(row_targets, col_targets, frame_rows):
    steps_range = jnp.arange(2 * RADIUS + 1, dtype=jnp.int32) - RADIUS
    positions = []
    masks_list = []
    offset = 0
    for level_no in range(LEVELS):
        factor = 2 ** level_no
        level_rows = frame_rows // factor
        level_cols = WC // factor
        owned_rows = RD // factor
        centre_row = row_targets // factor
        centre_col = col_targets // factor
        grid_row = centre_row[:, None, None, :] + steps_range[None, :, None, None]
        grid_col = centre_col[:, None, None, :] + steps_range[None, None, :, None]
        inside = (grid_row >= 0) & (grid_row < level_rows) & (grid_col >= 0) & (grid_col < level_cols)
        owner = grid_row // owned_rows
        within = grid_row - owner * owned_rows
        position = owner * PACK + offset + within * level_cols + grid_col
        positions.append(jnp.where(inside, position, 0))
        masks_list.append(inside)
        offset = offset + owned_rows * level_cols
    width_all = row_targets.shape[-1]
    position = jnp.stack(positions, 1).reshape(-1, width_all).astype(jnp.int32)
    inside = jnp.stack(masks_list, 1).reshape(-1, width_all)
    return (position, inside)

def encode_patches(padded, out_rows):
    taps = [padded[:, row_tap:row_tap + 2 * out_rows:2, col_tap:col_tap + 2 * WC:2, :] for row_tap in range(3) for col_tap in range(3)]
    return jnp.concatenate(taps, axis=-1)

def scatter_taps(grad_patches, out_rows):
    summed = jnp.zeros((2, 2 * out_rows + 1, 2 * WC + 2, C0), jnp.float32)
    for row_tap in range(3):
        for col_tap in range(3):
            summed = summed.at[:, row_tap:row_tap + 2 * out_rows:2, col_tap:col_tap + 2 * WC:2, :].add(grad_patches[:, :, :, row_tap, col_tap, :])
    return summed

def pool_levels(grid_map):
    shard_count = grid_map.shape[0]
    parts_list = []
    for level_no in range(LEVELS):
        factor = 2 ** level_no
        pooled = grid_map.astype(jnp.float32).reshape(shard_count, RD // factor, factor, WC // factor, factor, C).mean(axis=(2, 4))
        parts_list.append(pooled.astype(jnp.bfloat16).reshape(shard_count, RD // factor * (WC // factor), C))
    return jnp.concatenate(parts_list, axis=1).reshape(shard_count * PACK, C)

def spread_levels(own_cells):
    shard_count = own_cells.shape[0]
    summed = jnp.zeros((shard_count, RD, WC, C), jnp.float32)
    offset = 0
    for level_no in range(LEVELS):
        factor = 2 ** level_no
        level_rows = RD // factor
        level_cols = WC // factor
        segment = own_cells[:, offset:offset + level_rows * level_cols].reshape(shard_count, level_rows, 1, level_cols, 1, C)
        spread = jnp.broadcast_to(segment, (shard_count, level_rows, factor, level_cols, factor, C)).reshape(shard_count, RD, WC, C)
        summed = summed + spread / (factor * factor)
        offset = offset + level_rows * level_cols
    return summed.reshape(shard_count * RD * WC, C)

def reference(frames, conv_weight, conv_bias, proj_weight, target_row, target_col, cotangent):
    frame_rows = RD * N_ROWS
    pixel_count = frame_rows * WC
    pixels = RD * WC
    maps_view = frames.reshape(2, 2 * frame_rows, 2 * WC, C0)
    padded = jnp.pad(maps_view, ((0, 0), (1, 0), (1, 1), (0, 0)))
    patches = encode_patches(padded, frame_rows).reshape(2 * pixel_count, 9 * C0)
    preact = jnp.dot(patches, conv_weight, preferred_element_type=jnp.float32) + conv_bias
    hidden = jnp.maximum(preact, 0.0).astype(jnp.bfloat16)
    features = jnp.dot(hidden, proj_weight, preferred_element_type=jnp.float32).astype(jnp.bfloat16)
    first_map = features[:pixel_count]
    second_map = features[pixel_count:]
    pyramid = pool_levels(second_map.reshape(N_ROWS, RD, WC, C))
    inv_root = 1.0 / math.sqrt(C)
    column_ids = jnp.broadcast_to(jnp.arange(pixels, dtype=jnp.int32)[None, :], (LOOKS, pixels))

    def step_block(running, inputs):
        columns, rows_block, cols_block, cot_block = inputs
        position, inside = window_index(rows_block, cols_block, frame_rows)
        volume = jnp.dot(pyramid, columns.T, preferred_element_type=jnp.float32)
        picked = jnp.take_along_axis(volume, position, axis=0)
        looked = jnp.where(inside, picked * inv_root, 0.0).astype(jnp.bfloat16)
        hit_weights = jnp.where(inside, cot_block.astype(jnp.float32), 0.0)
        grad_volume = jnp.zeros(volume.shape, jnp.float32).at[position, column_ids].add(hit_weights).astype(jnp.bfloat16)
        grad_first = jnp.dot(grad_volume.T, pyramid, preferred_element_type=jnp.float32) * inv_root
        block_term = jnp.dot(grad_volume, columns, preferred_element_type=jnp.float32) * inv_root
        rounded = lax.optimization_barrier(block_term.astype(jnp.bfloat16))
        running = running + rounded.astype(jnp.float32)
        return (running, (looked, grad_first))
    block_inputs = (first_map.reshape(N_ROWS, pixels, C), target_row.reshape(ITERS, N_ROWS, pixels).transpose(1, 0, 2), target_col.reshape(ITERS, N_ROWS, pixels).transpose(1, 0, 2), cotangent.reshape(LOOKS, N_ROWS, pixels).transpose(1, 0, 2))
    start_sum = jnp.zeros((N_ROWS * PACK, C), jnp.float32)
    partial_value, (looked, grad_first) = lax.scan(step_block, start_sum, block_inputs)
    lookups = looked.transpose(1, 0, 2).reshape(LOOKS, pixel_count)
    grad_second = spread_levels(partial_value.reshape(N_ROWS, PACK, C))
    grad_feats = jnp.concatenate([grad_first.reshape(pixel_count, C), grad_second], axis=0).astype(jnp.bfloat16)
    grad_proj = lax.dot_general(hidden, grad_feats, (((0,), (0,)), ((), ())), preferred_element_type=jnp.float32)
    grad_hidden = lax.dot_general(grad_feats, proj_weight, (((1,), (1,)), ((), ())), preferred_element_type=jnp.float32)
    grad_preact = jnp.where(preact > 0.0, grad_hidden, 0.0).astype(jnp.bfloat16)
    grad_bias = lax.optimization_barrier(jnp.sum(grad_preact.astype(jnp.float32), axis=0))
    grad_conv = lax.dot_general(patches, grad_preact, (((0,), (0,)), ((), ())), preferred_element_type=jnp.float32)
    grad_patches = lax.dot_general(grad_preact, conv_weight, (((1,), (1,)), ((), ())), preferred_element_type=jnp.float32).reshape(2, frame_rows, WC, 3, 3, C0)
    grad_padded = scatter_taps(grad_patches, frame_rows)
    grad_input = grad_padded[:, 1:, 1:2 * WC + 1, :].reshape(2, 2 * frame_rows, 2 * WC * C0).astype(jnp.bfloat16)
    return (lookups, grad_input, grad_conv, grad_bias, grad_proj)
```

```python
import functools

import jax
import jax.numpy as jnp
from jax import lax
from jax.experimental import pallas as pl
from jax.experimental.pallas import tpu as pltpu
from jax.sharding import PartitionSpec as P

C = 256
C1 = 128
C0 = 96
LEVELS = 4
SPAN = 9
ITERS = 12
RD = 8
WC = 16
LOOKS = 3888
PIX = RD * WC
WIN = 384
F32 = jnp.float32
BF16 = jnp.bfloat16
VMEM = pltpu.CompilerParams(vmem_limit_bytes=56 * 1024 * 1024)

def dot(a, b):
    return jnp.dot(a, b, preferred_element_type=F32)

def dot_nt(a, b):
    return lax.dot_general(a, b, (((1,), (1,)), ((), ())), preferred_element_type=F32)

def dot_tn(a, b):
    return lax.dot_general(a, b, (((0,), (0,)), ((), ())), preferred_element_type=F32)

def iota(shape, dim):
    return lax.broadcasted_iota(jnp.int32, shape, dim)

def pick(tile, index):
    return jnp.take_along_axis(tile, index, axis=0, mode="promise_in_bounds")

def pool_matrix(ny):
    parts = []
    for level in range(1, LEVELS):
        shape = (ny >> level, ny)
        hit = iota(shape, 0) == (iota(shape, 1) >> level)
        parts.append(jnp.where(hit, 0.25**level, 0.0))
    return jnp.concatenate(parts, axis=0).astype(BF16)

def spread_matrix(ny):
    parts = []
    for level in range(1, LEVELS):
        shape = (ny, ny >> level)
        hit = (iota(shape, 0) >> level) == iota(shape, 1)
        parts.append(jnp.where(hit, 0.25**level, 0.0))
    return jnp.concatenate(parts, axis=1).astype(BF16)

def lane_row(ref, step):
    return jnp.broadcast_to(ref[pl.ds(step, 1), :], (8, PIX))

def place_columns(source, offset, cols):
    values = list(source)
    bit = 1
    while bit < cols:
        taken = (offset & bit) != 0
        last = 2 * bit >= cols
        size = len(values)
        moved = []
        for k in range(size + bit):
            if last and not 4 <= k < cols + 4:
                moved.append(None)
                continue
            here = values[k] if k < size else None
            back = values[k - bit] if 0 <= k - bit < size else None
            here = jnp.zeros((8, PIX), F32) if here is None else here
            back = jnp.zeros((8, PIX), F32) if back is None else back
            moved.append(jnp.where(taken, back, here))
        values = moved
        bit *= 2
    return values[4 : cols + 4]

def window_columns(source, offset, cols):
    zero = jnp.zeros((8, PIX), F32)
    values = [zero] * 4 + list(source) + [zero] * 4
    bit = cols // 2
    while bit >= 1:
        taken = (offset & bit) != 0
        values = [jnp.where(taken, values[k + bit], values[k]) for k in range(bit + 8)]
        bit //= 2
    return values

def scatter_kernel(ny, row_ref, col_ref, cot_ref, w_ref, grad_ref, grad_t_ref, wv_ref, cot, *sums):
    sub = iota((8, PIX), 0)
    cot[...] = cot_ref[...].astype(F32)
    for level in range(LEVELS):
        sums[level][...] = jnp.zeros(sums[level].shape, F32)
    wv_ref[...] = jnp.zeros(wv_ref.shape, BF16)
    for tap in range(3):
        lanes = slice(tap * C1, tap * C1 + C1)
        rows = w_ref[tap * 288 : tap * 288 + 288, :]
        wv_ref[0, 0:192, lanes] = rows[96:288]
        wv_ref[1, 96:384, lanes] = rows
        wv_ref[2, 32:320, lanes] = rows

    def step(t, carry):
        row_all, col_all = lane_row(row_ref, t), lane_row(col_ref, t)
        for level in range(LEVELS):
            cols, tiles = WC >> level, ny >> (level + 3)
            base = t * 324 + level * 81
            start = (row_all >> level) + 4
            col = col_all >> level
            shift, tile_at = start & 7, start >> 3
            body = [cot[pl.ds(base + dx, 8, stride=SPAN), :] for dx in range(SPAN)]
            tail = [
                jnp.broadcast_to(cot[pl.ds(base + 72 + dx, 1), :], (8, PIX)) for dx in range(SPAN)
            ]
            body = place_columns(body, col, cols)
            tail = place_columns(tail, col, cols)
            index = (sub - shift) & 7
            upper, lower, edge = sub >= shift, sub < shift, sub == shift
            hits = [tile_at == k for k in range(tiles + 1)]
            for v in range(cols):
                turned = pick(body[v], index)
                high = jnp.where(upper, turned, 0.0)
                low = jnp.where(lower, turned, jnp.where(edge, tail[v], 0.0))
                for k in range(tiles):
                    term = jnp.where(hits[k + 1], high, jnp.where(hits[k], low, 0.0))
                    sums[level][v, 8 * k : 8 * k + 8, :] += term
        return carry

    lax.fori_loop(0, ITERS, step, 0)
    spread = spread_matrix(ny)
    for pair in range(WC // 2):
        stacked = jnp.concatenate(
            [sums[level][pair >> (level - 1)] for level in range(1, LEVELS)], axis=0
        ).astype(BF16)
        added = dot(spread, stacked)
        for v in (2 * pair, 2 * pair + 1):
            total = sums[0][v] + added
            grad_ref[v] = total.astype(BF16)
            grad_t_ref[:, v * ny : v * ny + ny] = total.T.astype(BF16)

def scatter(ny, target_row, target_col, cotangent, conv_weight):
    return pl.pallas_call(
        functools.partial(scatter_kernel, ny),
        out_shape=(
            jax.ShapeDtypeStruct((WC, ny, PIX), BF16),
            jax.ShapeDtypeStruct((PIX, WC * ny), BF16),
            jax.ShapeDtypeStruct((3, WIN, WIN), BF16),
        ),
        scratch_shapes=[pltpu.VMEM((LOOKS, PIX), F32)]
        + [pltpu.VMEM((WC >> level, ny >> level, PIX), F32) for level in range(LEVELS)],
        compiler_params=VMEM,
        cost_estimate=pl.CostEstimate(flops=10**9, bytes_accessed=4 * 10**6, transcendentals=0),
        name="scatter",
    )(target_row, target_col, cotangent, conv_weight)

def lookup_kernel(ny, row_ref, col_ref, hid_ref, first_ref, proj_ref, out_ref, looked, *volumes):
    sub = iota((8, PIX), 0)
    first, proj = first_ref[...], proj_ref[...]
    pool = pool_matrix(ny)
    zero = jnp.zeros((8, PIX), F32)
    for level in range(LEVELS):
        for v in range(WC >> level):
            volumes[level][v, 0:8, :] = zero
            volumes[level][v, 8 + (ny >> level) :, :] = zero
    held = [None] * LEVELS
    for v in range(WC):
        second = dot(hid_ref[v], proj).astype(BF16)
        volumes[0][v, 8 : 8 + ny, :] = dot_nt(second, first) * (1.0 / 16.0)
        pooled = dot(pool, second)
        at = 0
        for level in range(1, LEVELS):
            part = pooled[at : at + (ny >> level)]
            at += ny >> level
            held[level] = part if v % (1 << level) == 0 else held[level] + part
            if (v + 1) % (1 << level) == 0:
                volumes[level][v >> level, 8 : 8 + (ny >> level), :] = dot_nt(
                    held[level].astype(BF16), first
                ) * (1.0 / 16.0)

    def step(t, carry):
        row_all, col_all = lane_row(row_ref, t), lane_row(col_ref, t)
        for level in range(LEVELS):
            cols, tiles = WC >> level, ny >> (level + 3)
            base = t * 324 + level * 81
            start = (row_all >> level) + 4
            col = col_all >> level
            shift, tile_at = start & 7, start >> 3
            index = (sub + shift) & 7
            upper = sub >= shift
            beyond = tile_at >= tiles
            body, tail = [], []
            for v in range(cols):
                held = [volumes[level][v, 8 * k : 8 * k + 8, :] for k in range(tiles + 2)]
                for k in range(2):
                    held[k] = jnp.where(beyond, held[tiles + k], held[k])
                bit = tiles // 2
                while bit >= 1:
                    taken = (tile_at & bit) != 0
                    held = [jnp.where(taken, held[k + bit], held[k]) for k in range(bit + 1)]
                    bit //= 2
                body.append(pick(jnp.where(upper, held[0], held[1]), index))
                tail.append(pick(held[1], shift))
            body = window_columns(body, col, cols)
            tail = window_columns(tail, col, cols)
            for dx in range(SPAN):
                looked[pl.ds(base + dx, 8, stride=SPAN), :] = body[dx]
                looked[pl.ds(base + 72 + dx, 1), :] = tail[dx][0:1]
        return carry

    lax.fori_loop(0, ITERS, step, 0)
    out_ref[...] = looked[...].astype(BF16)

def lookup(ny, target_row, target_col, hid, first, proj_weight):
    return pl.pallas_call(
        functools.partial(lookup_kernel, ny),
        out_shape=jax.ShapeDtypeStruct((LOOKS, PIX), BF16),
        scratch_shapes=[pltpu.VMEM((LOOKS, PIX), F32)]
        + [pltpu.VMEM((WC >> level, (ny >> level) + 16, PIX), F32) for level in range(LEVELS)],
        compiler_params=VMEM,
        cost_estimate=pl.CostEstimate(flops=10**9, bytes_accessed=4 * 10**6, transcendentals=0),
        name="lookup",
    )(target_row, target_col, hid, first, proj_weight)


def reverse_bits(value, bits):
    total = 0
    for bit in range(bits):
        total = total | (((value >> bit) & 1) << (bits - 1 - bit))
    return total


def window_of(c):
    if c == 0:
        return 0, 0
    return (1, 192 * (c - 1)) if c % 2 else (2, 192 * c - 128)


def row_pick(me, count, bits, half, parity):
    shape = (count * RD, count * RD)
    row, at = iota(shape, 0), iota(shape, 1)
    place = reverse_bits((row >> 3) ^ me, bits) * (2 * RD) + 2 * (row & 7) + parity
    return jnp.where(place == at + half * count * RD, 1.0, 0.0).astype(BF16)


def own_pick(shift, parity):
    shape = (2 * RD, 2 * RD)
    row, at = iota(shape, 0) - shift, iota(shape, 1)
    hit = (row >= 0) & (row < RD) & (at == 2 * row + parity)
    return jnp.where(hit, 1.0, 0.0).astype(BF16)


def pixel_pick(transposed):
    a, b = iota((PIX, PIX), 0), iota((PIX, PIX), 1)
    a, b = (b, a) if transposed else (a, b)
    return jnp.where(a == (b & 7) * WC + (b >> 3), 1.0, 0.0).astype(BF16)


def taps_outer(weights):
    return jnp.concatenate([weights[:, 0:C1], weights[:, 2 * C1 : 3 * C1]], axis=1)


def main_kernel(
    count, bits, share, me_ref, near_ref, far_ref, own_ref, halo_ref, wv_ref, bias_ref, proj_ref,
    grad_ref, grad_t_ref, sums_ref, hid_ref, first_ref, first_grad_ref, even, odd, moved, pre0, wsum
):
    ny = count * RD
    ext = ny + 2 * RD
    me = me_ref[0]
    picks = [[row_pick(me, count, bits, half, parity) for half in range(2)] for parity in range(2)]
    own = own_ref[...]
    for parity, dest in ((0, even), (1, odd)):
        for j in range(8):
            lanes = slice(j * WIN, j * WIN + WIN)
            dest[0:ny, lanes] = (
                dot(picks[parity][0], near_ref[:, lanes]) + dot(picks[parity][1], far_ref[:, lanes])
            ).astype(BF16)
    even[ny:ext, :] = dot(own_pick(0, 0), own).astype(BF16)
    tail = dot(own_pick(1, 1), own)
    top = jnp.broadcast_to(halo_ref[...].astype(F32), tail.shape)
    odd[ny:ext, :] = jnp.where(iota(tail.shape, 0) == 0, top, tail).astype(BF16)

    bias = bias_ref[...]
    moved[0:8, :] = jnp.zeros((8, 2 * C1), F32)
    for c in range(WC):
        variant, start = window_of(c)
        lanes = slice(start, start + WIN)
        inner = dot(even[:, lanes], wv_ref[variant, :, C1 : 2 * C1])
        outer = dot(odd[:, lanes], taps_outer(wv_ref[variant]))
        moved[8 : 8 + ext, :] = outer
        preact = inner[0:ny] + outer[0:ny, C1:] + moved[7 : 7 + ny, 0:C1] + bias
        hid_ref[c] = jnp.maximum(preact, 0.0).astype(BF16)
        pre0[8 * c : 8 * c + 8, :] = (
            inner[ny : ny + 8]
            + outer[ny : ny + 8, 0:C1]
            + moved[8 + ny + 1 : 8 + ny + 9, C1:]
            + bias
        )

    proj = proj_ref[...]
    hid0 = dot(pixel_pick(False), jnp.maximum(pre0[...], 0.0).astype(BF16)).astype(BF16)
    first = dot(hid0, proj).astype(BF16)
    first_ref[...] = first
    mixed = (dot(grad_t_ref[...], hid_ref[...].reshape(WC * ny, C1)) * (1.0 / 16.0)).astype(BF16)
    grad_first = dot(mixed, proj).astype(BF16)
    grad_proj = dot_tn(mixed, first) + dot_tn(hid0, grad_first)
    pre_grad0 = dot(pixel_pick(True), dot_nt(grad_first, proj).astype(BF16))
    pre_grad0 = jnp.where(pre0[...] > 0.0, pre_grad0, 0.0)
    first_grad_ref[...] = pre_grad0.astype(BF16)
    pre0[...] = pre_grad0
    fold = (dot_nt(first, proj) * (1.0 / 16.0)).astype(BF16)

    bias_sum = jnp.sum(pre_grad0, axis=0, keepdims=True)
    totals_in, totals_out = [None] * 3, [None] * 3
    zeros8 = jnp.zeros((8, C1), F32)
    previous = None
    for c in range(WC):
        variant, start = window_of(c)
        lanes = slice(start, start + WIN)
        grad = jnp.where(hid_ref[c].astype(F32) > 0.0, dot(grad_ref[c], fold), 0.0)
        own_grad = pre0[8 * c : 8 * c + 8, :]
        bias_sum = bias_sum + jnp.sum(grad, axis=0, keepdims=True)
        moved[0:ny, 0:C1] = grad
        moved[ny : ny + 8, 0:C1] = zeros8
        shifted_grad = moved[1 : 1 + ny, 0:C1]
        moved[ny : ny + 8, C1:] = zeros8
        moved[ny + 8 : ny + 16, C1:] = zeros8
        moved[ny + 1 : ny + 9, C1:] = own_grad
        late = moved[ny : ny + 16, C1:]
        inner = jnp.concatenate([grad, own_grad, zeros8], axis=0).astype(BF16)
        outer = jnp.concatenate(
            [
                jnp.concatenate([shifted_grad, own_grad, zeros8], axis=0),
                jnp.concatenate([grad, late], axis=0),
            ],
            axis=1,
        ).astype(BF16)
        part_in = dot_tn(inner, even[:, lanes])
        part_out = dot_tn(outer, odd[:, lanes])
        if totals_in[variant] is None:
            totals_in[variant], totals_out[variant] = part_in, part_out
        else:
            totals_in[variant] = totals_in[variant] + part_in
            totals_out[variant] = totals_out[variant] + part_out
        if c % 2:
            for d in range(count):
                pair = [g[8 * d : 8 * d + 8] for g in (previous, grad)]
                sums_ref[reverse_bits(d, bits), 8 * (c - 1) : 8 * (c + 1), :] = jnp.concatenate(
                    pair, axis=0
                ).astype(BF16)
        previous = grad

    wsum[9 * C0 + 2 * C1 :, :] = jnp.zeros((count * share - 9 * C0 - 2 * C1, C1), F32)
    for tap in range(3):
        if tap == 1:
            parts = totals_in
        else:
            at = 0 if tap == 0 else C1
            parts = [t[at : at + C1] for t in totals_out]
        parts = [p.T for p in parts]
        whole = parts[1][96:384] + parts[2][32:320]
        wsum[tap * 288 : tap * 288 + 96, :] = whole[0:96]
        wsum[tap * 288 + 96 : tap * 288 + 288, :] = whole[96:288] + parts[0][0:192]
    wsum[9 * C0 : 9 * C0 + C1, :] = grad_proj[:, 0:C1]
    wsum[9 * C0 + C1 : 9 * C0 + 2 * C1, :] = grad_proj[:, C1:]
    wsum[9 * C0 + 2 * C1 : 9 * C0 + 2 * C1 + 1, :] = bias_sum
    for p in range(count):
        sums_ref[p, PIX : PIX + share, :] = wsum[share * p : share * p + share, :].astype(BF16)


def whole(*shape):
    return pl.BlockSpec(shape, lambda: (0,) * len(shape))


def main(count, bits, share, me, near, far, own, halo, wv, bias, proj_weight, grad, grad_t):
    ny = count * RD
    ext = ny + 2 * RD
    vmem = pl.BlockSpec(memory_space=pltpu.VMEM)
    return pl.pallas_call(
        functools.partial(main_kernel, count, bits, share),
        in_specs=[pl.BlockSpec(memory_space=pltpu.SMEM)] + [vmem] * 9,
        out_shape=(
            jax.ShapeDtypeStruct((count, PIX + share, C1), BF16),
            jax.ShapeDtypeStruct((WC, ny, C1), BF16),
            jax.ShapeDtypeStruct((PIX, C), BF16),
            jax.ShapeDtypeStruct((PIX, C1), BF16),
        ),
        scratch_shapes=[
            pltpu.VMEM((ext, 2 * WC * C0), BF16),
            pltpu.VMEM((ext, 2 * WC * C0), BF16),
            pltpu.VMEM((ext + 16, 2 * C1), F32),
            pltpu.VMEM((PIX, C1), F32),
            pltpu.VMEM((count * share, C1), F32),
        ],
        compiler_params=VMEM,
        cost_estimate=pl.CostEstimate(flops=4 * 10**9, bytes_accessed=6 * 10**6, transcendentals=0),
        name="features",
    )(me, near, far, own, halo, wv, bias, proj_weight, grad, grad_t)


def input_kernel(first_ref, second_ref, border_ref, wv_ref, out_ref, sides, full):
    last = iota((8, C1), 0) == 7
    border = border_ref[...].astype(F32)
    grads = [first_ref[...].astype(F32), second_ref[...].astype(F32)]

    def stacked(columns):
        here, both = [], []
        for c in columns:
            for f in range(2):
                own = grads[f][8 * c : 8 * c + 8]
                below = jnp.broadcast_to(border[f * WC + c : f * WC + c + 1], (8, C1))
                here.append(own)
                both.append(
                    jnp.concatenate([own, jnp.where(last, below, pltpu.roll(own, 7, 0))], axis=1)
                )
        return jnp.concatenate(here, axis=0).astype(BF16), jnp.concatenate(both, axis=0).astype(BF16)

    def spread(columns, variant):
        here, both = stacked(columns)
        weights = wv_ref[variant]
        outer = jnp.concatenate([weights[:, 2 * C1 : 3 * C1], weights[:, 0:C1]], axis=1)
        return dot_nt(here, weights[:, C1 : 2 * C1]), dot_nt(both, outer)

    odd = spread(range(1, WC, 2), 1)
    even = spread(range(2, WC, 2), 2)
    edge = spread([0], 0)
    for parity in range(2):
        for q in range(8):
            sides[parity, :, q * WIN : q * WIN + WIN] = odd[parity][16 * q : 16 * q + 16]
        for q in range(1, 8):
            sides[parity, :, q * WIN - 128 : q * WIN + 256] += even[parity][16 * q - 16 : 16 * q]
        sides[parity, :, 0:WIN] += edge[parity]
        for f in range(2):
            for j in range(2 * WC * C0 // 128):
                lanes = slice(128 * j, 128 * j + 128)
                full[f, j, pl.ds(parity, 8, stride=2), :] = sides[parity, 8 * f : 8 * f + 8, lanes]
    for f in range(2):
        for j in range(2 * WC * C0 // 128):
            out_ref[f, :, 128 * j : 128 * j + 128] = full[f, j].astype(BF16)


def input_grad(first_grad, second_grad, border, wv):
    return pl.pallas_call(
        input_kernel,
        out_shape=jax.ShapeDtypeStruct((2, 2 * RD, 2 * WC * C0), BF16),
        scratch_shapes=[
            pltpu.VMEM((2, 2 * RD, 2 * WC * C0), F32),
            pltpu.VMEM((2, 2 * WC * C0 // 128, 2 * RD, 128), F32),
        ],
        compiler_params=VMEM,
        cost_estimate=pl.CostEstimate(flops=10**8, bytes_accessed=10**6, transcendentals=0),
        name="input_grad",
    )(first_grad, second_grad, border, wv)


def final_kernel(count, bits, share, me_ref, near_ref, far_ref, conv_ref, bias_ref, proj_ref, wsum):
    turned = reverse_bits(me_ref[0], bits)
    for half, ref in ((0, near_ref), (1, far_ref)):
        for j in range(count // 2):
            at = (turned ^ (half * (count // 2) + j)) * share
            wsum[pl.ds(pl.multiple_of(at, 16), share), :] = ref[j].astype(F32)
    conv_ref[...] = wsum[0 : 9 * C0, :]
    proj_ref[:, 0:C1] = wsum[9 * C0 : 9 * C0 + C1, :]
    proj_ref[:, C1:] = wsum[9 * C0 + C1 : 9 * C0 + 2 * C1, :]
    bias_ref[...] = wsum[9 * C0 + 2 * C1 : 9 * C0 + 2 * C1 + 1, :]


def final(count, bits, share, me, near, far):
    vmem = pl.BlockSpec(memory_space=pltpu.VMEM)
    return pl.pallas_call(
        functools.partial(final_kernel, count, bits, share),
        in_specs=[pl.BlockSpec(memory_space=pltpu.SMEM), vmem, vmem],
        out_shape=(
            jax.ShapeDtypeStruct((9 * C0, C1), F32),
            jax.ShapeDtypeStruct((1, C1), F32),
            jax.ShapeDtypeStruct((C1, C), F32),
        ),
        scratch_shapes=[pltpu.VMEM((count * share, C1), F32)],
        compiler_params=VMEM,
        name="weight_grads",
    )(me, near, far)


def swap(value, bit, count):
    return lax.ppermute(value, "rows", [(i, i ^ bit) for i in range(count)])


def per_device(frames, conv_weight, conv_bias, proj_weight, target_row, target_col, cotangent):
    count = lax.axis_size("rows")
    bits = count.bit_length() - 1
    ny = count * RD
    me = lax.axis_index("rows").astype(jnp.int32)
    me_word = me.reshape(1)
    share = -(-(9 * C0 + 2 * C1 + 1) // (16 * count)) * 16

    halo = lax.ppermute(frames[0, 2 * RD - 1 :], "rows", [(i, i + 1) for i in range(count - 1)])
    near = frames[1]
    far = None
    for bit in reversed(range(bits)):
        if far is not None:
            near = jnp.concatenate([near, far], axis=0)
        far = swap(near, 1 << bit, count)
    grad, grad_t, wv = scatter(ny, target_row, target_col, cotangent, conv_weight)
    sums, hid, first, first_grad = main(
        count, bits, share, me_word, near, far, frames[0], halo, wv,
        conv_bias.reshape(1, C1), proj_weight, grad, grad_t,
    )
    for bit in range(bits):
        half = sums.shape[0] // 2
        mine = (me >> bit) & 1
        kept = lax.dynamic_slice_in_dim(sums, mine * half, half, 0)
        sent = lax.dynamic_slice_in_dim(sums, (1 - mine) * half, half, 0)
        sums = (kept.astype(F32) + swap(sent, 1 << bit, count).astype(F32)).astype(BF16)
    second_grad = sums[0, :PIX]
    tops = jnp.concatenate([first_grad, second_grad], axis=0).reshape(2 * WC, RD, C1)[:, 0]
    border = lax.ppermute(tops, "rows", [(i + 1, i) for i in range(count - 1)])
    near = sums[:, PIX:]
    far = None
    for bit in reversed(range(bits)):
        if far is not None:
            near = jnp.concatenate([near, far], axis=0)
        far = swap(near, 1 << bit, count)
    grad_conv, grad_bias, grad_proj = final(count, bits, share, me_word, near, far)
    grad_input = input_grad(first_grad, second_grad, border, wv)
    lookups = lookup(ny, target_row, target_col, hid, first, proj_weight)
    return lookups, grad_input, grad_conv, grad_bias.reshape(C1), grad_proj


def solution(mesh):
    split = P(None, ("pairs", "rows"))
    return jax.shard_map(
        per_device,
        mesh=mesh,
        in_specs=(P(None, ("pairs", "rows"), None), P(), P(), P(), split, split, split),
        out_specs=(
            split,
            P(None, ("pairs", "rows"), None),
            P("pairs", None),
            P("pairs"),
            P("pairs", None),
        ),
        check_vma=False,
    )
```

```python
import functools

import jax
import jax.numpy as jnp
from jax import lax
from jax.experimental import pallas as pl
from jax.experimental.pallas import tpu as pltpu
from jax.sharding import PartitionSpec as P

C = 256
C1 = 128
C0 = 96
LEVELS = 4
SPAN = 9
ITERS = 12
RD = 8
WC = 16
LOOKS = 3888
PIX = RD * WC
WIN = 384
F32 = jnp.float32
BF16 = jnp.bfloat16
VMEM = pltpu.CompilerParams(vmem_limit_bytes=56 * 1024 * 1024)

def dot(a, b):
    return jnp.dot(a, b, preferred_element_type=F32)

def dot_nt(a, b):
    return lax.dot_general(a, b, (((1,), (1,)), ((), ())), preferred_element_type=F32)

def dot_tn(a, b):
    return lax.dot_general(a, b, (((0,), (0,)), ((), ())), preferred_element_type=F32)

def iota(shape, dim):
    return lax.broadcasted_iota(jnp.int32, shape, dim)

def pick(tile, index):
    return jnp.take_along_axis(tile, index, axis=0, mode="promise_in_bounds")

def pool_matrix(ny):
    parts = []
    for level in range(1, LEVELS):
        shape = (ny >> level, ny)
        hit = iota(shape, 0) == (iota(shape, 1) >> level)
        parts.append(jnp.where(hit, 0.25**level, 0.0))
    return jnp.concatenate(parts, axis=0).astype(BF16)

def spread_matrix(ny):
    parts = []
    for level in range(1, LEVELS):
        shape = (ny, ny >> level)
        hit = (iota(shape, 0) >> level) == iota(shape, 1)
        parts.append(jnp.where(hit, 0.25**level, 0.0))
    return jnp.concatenate(parts, axis=1).astype(BF16)

def lane_row(ref, step):
    return jnp.broadcast_to(ref[pl.ds(step, 1), :], (8, PIX))

def place_columns(source, offset, cols):
    values = list(source)
    bit = 1
    while bit < cols:
        taken = (offset & bit) != 0
        last = 2 * bit >= cols
        size = len(values)
        moved = []
        for k in range(size + bit):
            if last and not 4 <= k < cols + 4:
                moved.append(None)
                continue
            here = values[k] if k < size else None
            back = values[k - bit] if 0 <= k - bit < size else None
            here = jnp.zeros((8, PIX), F32) if here is None else here
            back = jnp.zeros((8, PIX), F32) if back is None else back
            moved.append(jnp.where(taken, back, here))
        values = moved
        bit *= 2
    return values[4 : cols + 4]

def window_columns(source, offset, cols):
    zero = jnp.zeros((8, PIX), F32)
    values = [zero] * 4 + list(source) + [zero] * 4
    bit = cols // 2
    while bit >= 1:
        taken = (offset & bit) != 0
        values = [jnp.where(taken, values[k + bit], values[k]) for k in range(bit + 8)]
        bit //= 2
    return values

def scatter_kernel(ny, row_ref, col_ref, cot_ref, w_ref, grad_ref, grad_t_ref, wv_ref, cot, *sums):
    sub = iota((8, PIX), 0)
    cot[...] = cot_ref[...].astype(F32)
    for level in range(LEVELS):
        sums[level][...] = jnp.zeros(sums[level].shape, F32)
    wv_ref[...] = jnp.zeros(wv_ref.shape, BF16)
    for tap in range(3):
        lanes = slice(tap * C1, tap * C1 + C1)
        rows = w_ref[tap * 288 : tap * 288 + 288, :]
        wv_ref[0, 0:192, lanes] = rows[96:288]
        wv_ref[1, 96:384, lanes] = rows
        wv_ref[2, 32:320, lanes] = rows

    def step(t, carry):
        row_all, col_all = lane_row(row_ref, t), lane_row(col_ref, t)
        for level in range(LEVELS):
            cols, tiles = WC >> level, ny >> (level + 3)
            base = t * 324 + level * 81
            start = (row_all >> level) + 4
            col = col_all >> level
            shift, tile_at = start & 7, start >> 3
            body = [cot[pl.ds(base + dx, 8, stride=SPAN), :] for dx in range(SPAN)]
            tail = [
                jnp.broadcast_to(cot[pl.ds(base + 72 + dx, 1), :], (8, PIX)) for dx in range(SPAN)
            ]
            body = place_columns(body, col, cols)
            tail = place_columns(tail, col, cols)
            index = (sub - shift) & 7
            upper, lower, edge = sub >= shift, sub < shift, sub == shift
            hits = [tile_at == k for k in range(tiles + 1)]
            for v in range(cols):
                turned = pick(body[v], index)
                high = jnp.where(upper, turned, 0.0)
                low = jnp.where(lower, turned, jnp.where(edge, tail[v], 0.0))
                for k in range(tiles):
                    term = jnp.where(hits[k + 1], high, jnp.where(hits[k], low, 0.0))
                    sums[level][v, 8 * k : 8 * k + 8, :] += term
        return carry

    lax.fori_loop(0, ITERS, step, 0)
    spread = spread_matrix(ny)
    for pair in range(WC // 2):
        stacked = jnp.concatenate(
            [sums[level][pair >> (level - 1)] for level in range(1, LEVELS)], axis=0
        ).astype(BF16)
        added = dot(spread, stacked)
        for v in (2 * pair, 2 * pair + 1):
            total = sums[0][v] + added
            grad_ref[v] = total.astype(BF16)
            grad_t_ref[:, v * ny : v * ny + ny] = total.T.astype(BF16)

def scatter(ny, target_row, target_col, cotangent, conv_weight):
    return pl.pallas_call(
        functools.partial(scatter_kernel, ny),
        out_shape=(
            jax.ShapeDtypeStruct((WC, ny, PIX), BF16),
            jax.ShapeDtypeStruct((PIX, WC * ny), BF16),
            jax.ShapeDtypeStruct((3, WIN, WIN), BF16),
        ),
        scratch_shapes=[pltpu.VMEM((LOOKS, PIX), F32)]
        + [pltpu.VMEM((WC >> level, ny >> level, PIX), F32) for level in range(LEVELS)],
        compiler_params=VMEM,
        cost_estimate=pl.CostEstimate(flops=10**9, bytes_accessed=4 * 10**6, transcendentals=0),
        name="scatter",
    )(target_row, target_col, cotangent, conv_weight)

def lookup_kernel(ny, row_ref, col_ref, hid_ref, first_ref, proj_ref, out_ref, looked, *volumes):
    sub = iota((8, PIX), 0)
    first, proj = first_ref[...], proj_ref[...]
    pool = pool_matrix(ny)
    zero = jnp.zeros((8, PIX), F32)
    for level in range(LEVELS):
        for v in range(WC >> level):
            volumes[level][v, 0:8, :] = zero
            volumes[level][v, 8 + (ny >> level) :, :] = zero
    held = [None] * LEVELS
    for v in range(WC):
        second = dot(hid_ref[v], proj).astype(BF16)
        volumes[0][v, 8 : 8 + ny, :] = dot_nt(second, first) * (1.0 / 16.0)
        pooled = dot(pool, second)
        at = 0
        for level in range(1, LEVELS):
            part = pooled[at : at + (ny >> level)]
            at += ny >> level
            held[level] = part if v % (1 << level) == 0 else held[level] + part
            if (v + 1) % (1 << level) == 0:
                volumes[level][v >> level, 8 : 8 + (ny >> level), :] = dot_nt(
                    held[level].astype(BF16), first
                ) * (1.0 / 16.0)

    def step(t, carry):
        row_all, col_all = lane_row(row_ref, t), lane_row(col_ref, t)
        for level in range(LEVELS):
            cols, tiles = WC >> level, ny >> (level + 3)
            base = t * 324 + level * 81
            start = (row_all >> level) + 4
            col = col_all >> level
            shift, tile_at = start & 7, start >> 3
            index = (sub + shift) & 7
            upper = sub >= shift
            beyond = tile_at >= tiles
            body, tail = [], []
            for v in range(cols):
                held = [volumes[level][v, 8 * k : 8 * k + 8, :] for k in range(tiles + 2)]
                for k in range(2):
                    held[k] = jnp.where(beyond, held[tiles + k], held[k])
                bit = tiles // 2
                while bit >= 1:
                    taken = (tile_at & bit) != 0
                    held = [jnp.where(taken, held[k + bit], held[k]) for k in range(bit + 1)]
                    bit //= 2
                body.append(pick(jnp.where(upper, held[0], held[1]), index))
                tail.append(pick(held[1], shift))
            body = window_columns(body, col, cols)
            tail = window_columns(tail, col, cols)
            for dx in range(SPAN):
                looked[pl.ds(base + dx, 8, stride=SPAN), :] = body[dx]
                looked[pl.ds(base + 72 + dx, 1), :] = tail[dx][0:1]
        return carry

    lax.fori_loop(0, ITERS, step, 0)
    out_ref[...] = looked[...].astype(BF16)

def lookup(ny, target_row, target_col, hid, first, proj_weight):
    return pl.pallas_call(
        functools.partial(lookup_kernel, ny),
        out_shape=jax.ShapeDtypeStruct((LOOKS, PIX), BF16),
        scratch_shapes=[pltpu.VMEM((LOOKS, PIX), F32)]
        + [pltpu.VMEM((WC >> level, (ny >> level) + 16, PIX), F32) for level in range(LEVELS)],
        compiler_params=VMEM,
        cost_estimate=pl.CostEstimate(flops=10**9, bytes_accessed=4 * 10**6, transcendentals=0),
        name="lookup",
    )(target_row, target_col, hid, first, proj_weight)


def reverse_bits(value, bits):
    total = 0
    for bit in range(bits):
        total = total | (((value >> bit) & 1) << (bits - 1 - bit))
    return total


def window_of(c):
    if c == 0:
        return 0, 0
    return (1, 192 * (c - 1)) if c % 2 else (2, 192 * c - 128)


def row_pick(me, count, bits, half, parity):
    shape = (count * RD, count * RD)
    row, at = iota(shape, 0), iota(shape, 1)
    place = reverse_bits((row >> 3) ^ me, bits) * (2 * RD) + 2 * (row & 7) + parity
    return jnp.where(place == at + half * count * RD, 1.0, 0.0).astype(BF16)


def own_pick(shift, parity):
    shape = (2 * RD, 2 * RD)
    row, at = iota(shape, 0) - shift, iota(shape, 1)
    hit = (row >= 0) & (row < RD) & (at == 2 * row + parity)
    return jnp.where(hit, 1.0, 0.0).astype(BF16)


def pixel_pick(transposed):
    a, b = iota((PIX, PIX), 0), iota((PIX, PIX), 1)
    a, b = (b, a) if transposed else (a, b)
    return jnp.where(a == (b & 7) * WC + (b >> 3), 1.0, 0.0).astype(BF16)


def taps_outer(weights):
    return jnp.concatenate([weights[:, 0:C1], weights[:, 2 * C1 : 3 * C1]], axis=1)


def main_kernel(
    count, bits, quarter, me_ref, near_ref, far_ref, own_ref, halo_ref, wv_ref, bias_ref, proj_ref,
    grad_ref, grad_t_ref, kept_ref, sent_ref, hid_ref, first_ref, first_grad_ref, even, odd, moved, pre0,
    wsum, pair
):
    ny = count * RD
    ext = ny + 2 * RD
    me = me_ref[0]
    picks = [[row_pick(me, count, bits, half, parity) for half in range(2)] for parity in range(2)]
    own = own_ref[...]
    for parity, dest in ((0, even), (1, odd)):
        for j in range(8):
            lanes = slice(j * WIN, j * WIN + WIN)
            dest[0:ny, lanes] = (
                dot(picks[parity][0], near_ref[:, lanes]) + dot(picks[parity][1], far_ref[:, lanes])
            ).astype(BF16)
    even[ny:ext, :] = dot(own_pick(0, 0), own).astype(BF16)
    tail = dot(own_pick(1, 1), own)
    top = jnp.broadcast_to(halo_ref[...].astype(F32), tail.shape)
    odd[ny:ext, :] = jnp.where(iota(tail.shape, 0) == 0, top, tail).astype(BF16)

    bias = bias_ref[...]
    moved[0:8, :] = jnp.zeros((8, 2 * C1), F32)
    for c in range(WC):
        variant, start = window_of(c)
        lanes = slice(start, start + WIN)
        inner = dot(even[:, lanes], wv_ref[variant, :, C1 : 2 * C1])
        outer = dot(odd[:, lanes], taps_outer(wv_ref[variant]))
        moved[8 : 8 + ext, :] = outer
        preact = inner[0:ny] + outer[0:ny, C1:] + moved[7 : 7 + ny, 0:C1] + bias
        hid_ref[c] = jnp.maximum(preact, 0.0).astype(BF16)
        pre0[8 * c : 8 * c + 8, :] = (
            inner[ny : ny + 8]
            + outer[ny : ny + 8, 0:C1]
            + moved[8 + ny + 1 : 8 + ny + 9, C1:]
            + bias
        )

    proj = proj_ref[...]
    hid0 = dot(pixel_pick(False), jnp.maximum(pre0[...], 0.0).astype(BF16)).astype(BF16)
    first = dot(hid0, proj).astype(BF16)
    first_ref[...] = first
    mixed = (dot(grad_t_ref[...], hid_ref[...].reshape(WC * ny, C1)) * (1.0 / 16.0)).astype(BF16)
    grad_first = dot(mixed, proj).astype(BF16)
    grad_proj = dot_tn(mixed, first) + dot_tn(hid0, grad_first)
    pre_grad0 = dot(pixel_pick(True), dot_nt(grad_first, proj).astype(BF16))
    pre_grad0 = jnp.where(pre0[...] > 0.0, pre_grad0, 0.0)
    first_grad_ref[...] = pre_grad0.astype(BF16)
    pre0[...] = pre_grad0
    fold = (dot_nt(first, proj) * (1.0 / 16.0)).astype(BF16)

    bias_sum = jnp.sum(pre_grad0, axis=0, keepdims=True)
    totals_in, totals_out = [None] * 3, [None] * 3
    zeros8 = jnp.zeros((8, C1), F32)
    for c in range(WC):
        variant, start = window_of(c)
        lanes = slice(start, start + WIN)
        grad = jnp.where(hid_ref[c].astype(F32) > 0.0, dot(grad_ref[c], fold), 0.0)
        own_grad = pre0[8 * c : 8 * c + 8, :]
        bias_sum = bias_sum + jnp.sum(grad, axis=0, keepdims=True)
        moved[0:ny, 0:C1] = grad
        moved[ny : ny + 8, 0:C1] = zeros8
        shifted_grad = moved[1 : 1 + ny, 0:C1]
        moved[ny : ny + 8, C1:] = zeros8
        moved[ny + 8 : ny + 16, C1:] = zeros8
        moved[ny + 1 : ny + 9, C1:] = own_grad
        late = moved[ny : ny + 16, C1:]
        inner = jnp.concatenate([grad, own_grad, zeros8], axis=0).astype(BF16)
        outer = jnp.concatenate(
            [
                jnp.concatenate([shifted_grad, own_grad, zeros8], axis=0),
                jnp.concatenate([grad, late], axis=0),
            ],
            axis=1,
        ).astype(BF16)
        part_in = dot_tn(inner, even[:, lanes])
        part_out = dot_tn(outer, odd[:, lanes])
        if totals_in[variant] is None:
            totals_in[variant], totals_out[variant] = part_in, part_out
        else:
            totals_in[variant] = totals_in[variant] + part_in
            totals_out[variant] = totals_out[variant] + part_out
        pair[c % 2] = grad
        if c % 2:
            for place in range(count):
                row = pl.multiple_of((reverse_bits(place, bits) ^ me) * RD, RD)
                rows = [pair[k, pl.ds(row, RD), :] for k in range(2)]
                dest = (kept_ref, sent_ref)[place // (count // 2)]
                block = place % (count // 4)
                at = PIX * block + RD * (c - 1)
                dest[place // (count // 4) % 2, at : at + 2 * RD, :] = jnp.concatenate(
                    rows, axis=0
                ).astype(BF16)

    wsum[9 * C0 + 2 * C1 :, :] = jnp.zeros((4 * quarter - 9 * C0 - 2 * C1, C1), F32)
    for tap in range(3):
        if tap == 1:
            parts = totals_in
        else:
            at = 0 if tap == 0 else C1
            parts = [t[at : at + C1] for t in totals_out]
        parts = [p.T for p in parts]
        whole = parts[1][96:384] + parts[2][32:320]
        wsum[tap * 288 : tap * 288 + 96, :] = whole[0:96]
        wsum[tap * 288 + 96 : tap * 288 + 288, :] = whole[96:288] + parts[0][0:192]
    wsum[9 * C0 : 9 * C0 + C1, :] = grad_proj[:, 0:C1]
    wsum[9 * C0 + C1 : 9 * C0 + 2 * C1, :] = grad_proj[:, C1:]
    wsum[9 * C0 + 2 * C1 : 9 * C0 + 2 * C1 + 1, :] = bias_sum
    for place in range(4):
        row = pl.multiple_of((place ^ reverse_bits(me & 3, 2)) * quarter, 16)
        dest = (kept_ref, sent_ref)[place // 2]
        dest[place % 2, PIX * count // 4 :, :] = wsum[pl.ds(row, quarter), :].astype(BF16)


def main(count, bits, quarter, me, near, far, own, halo, wv, bias, proj_weight, grad, grad_t):
    ny = count * RD
    ext = ny + 2 * RD
    vmem = pl.BlockSpec(memory_space=pltpu.VMEM)
    return pl.pallas_call(
        functools.partial(main_kernel, count, bits, quarter),
        in_specs=[pl.BlockSpec(memory_space=pltpu.SMEM)] + [vmem] * 9,
        out_shape=(
            jax.ShapeDtypeStruct((2, PIX * count // 4 + quarter, C1), BF16),
            jax.ShapeDtypeStruct((2, PIX * count // 4 + quarter, C1), BF16),
            jax.ShapeDtypeStruct((WC, ny, C1), BF16),
            jax.ShapeDtypeStruct((PIX, C), BF16),
            jax.ShapeDtypeStruct((PIX, C1), BF16),
        ),
        scratch_shapes=[
            pltpu.VMEM((ext, 2 * WC * C0), BF16),
            pltpu.VMEM((ext, 2 * WC * C0), BF16),
            pltpu.VMEM((ext + 16, 2 * C1), F32),
            pltpu.VMEM((PIX, C1), F32),
            pltpu.VMEM((4 * quarter, C1), F32),
            pltpu.VMEM((2, ny, C1), F32),
        ],
        compiler_params=VMEM,
        cost_estimate=pl.CostEstimate(flops=4 * 10**9, bytes_accessed=6 * 10**6, transcendentals=0),
        name="features",
    )(me, near, far, own, halo, wv, bias, proj_weight, grad, grad_t)


def input_kernel(first_ref, second_ref, border_ref, wv_ref, out_ref, sides, full):
    last = iota((8, C1), 0) == 7
    border = border_ref[...].astype(F32)
    grads = [first_ref[...].astype(F32), second_ref[...].astype(F32)]

    def stacked(columns):
        here, both = [], []
        for c in columns:
            for f in range(2):
                own = grads[f][8 * c : 8 * c + 8]
                below = jnp.broadcast_to(border[f * WC + c : f * WC + c + 1], (8, C1))
                here.append(own)
                both.append(
                    jnp.concatenate([own, jnp.where(last, below, pltpu.roll(own, 7, 0))], axis=1)
                )
        return jnp.concatenate(here, axis=0).astype(BF16), jnp.concatenate(both, axis=0).astype(BF16)

    def spread(columns, variant):
        here, both = stacked(columns)
        weights = wv_ref[variant]
        outer = jnp.concatenate([weights[:, 2 * C1 : 3 * C1], weights[:, 0:C1]], axis=1)
        return dot_nt(here, weights[:, C1 : 2 * C1]), dot_nt(both, outer)

    odd = spread(range(1, WC, 2), 1)
    even = spread(range(2, WC, 2), 2)
    edge = spread([0], 0)
    for parity in range(2):
        for q in range(8):
            sides[parity, :, q * WIN : q * WIN + WIN] = odd[parity][16 * q : 16 * q + 16]
        for q in range(1, 8):
            sides[parity, :, q * WIN - 128 : q * WIN + 256] += even[parity][16 * q - 16 : 16 * q]
        sides[parity, :, 0:WIN] += edge[parity]
        for f in range(2):
            for j in range(2 * WC * C0 // 128):
                lanes = slice(128 * j, 128 * j + 128)
                full[f, j, pl.ds(parity, 8, stride=2), :] = sides[parity, 8 * f : 8 * f + 8, lanes]
    for f in range(2):
        for j in range(2 * WC * C0 // 128):
            out_ref[f, :, 128 * j : 128 * j + 128] = full[f, j].astype(BF16)


def input_grad(first_grad, second_grad, border, wv):
    return pl.pallas_call(
        input_kernel,
        out_shape=jax.ShapeDtypeStruct((2, 2 * RD, 2 * WC * C0), BF16),
        scratch_shapes=[
            pltpu.VMEM((2, 2 * RD, 2 * WC * C0), F32),
            pltpu.VMEM((2, 2 * WC * C0 // 128, 2 * RD, 128), F32),
        ],
        compiler_params=VMEM,
        cost_estimate=pl.CostEstimate(flops=10**8, bytes_accessed=10**6, transcendentals=0),
        name="input_grad",
    )(first_grad, second_grad, border, wv)


def final_kernel(quarter, me_ref, near_ref, far_ref, conv_ref, bias_ref, proj_ref, wsum):
    turned = reverse_bits(me_ref[0] & 3, 2)
    for place in range(4):
        ref = (near_ref, far_ref)[place // 2]
        row = pl.multiple_of((place ^ turned) * quarter, 16)
        wsum[pl.ds(row, quarter), :] = ref[place % 2].astype(F32)
    conv_ref[...] = wsum[0 : 9 * C0, :]
    proj_ref[:, 0:C1] = wsum[9 * C0 : 9 * C0 + C1, :]
    proj_ref[:, C1:] = wsum[9 * C0 + C1 : 9 * C0 + 2 * C1, :]
    bias_ref[...] = wsum[9 * C0 + 2 * C1 : 9 * C0 + 2 * C1 + 1, :]


def final(quarter, me, near, far):
    vmem = pl.BlockSpec(memory_space=pltpu.VMEM)
    return pl.pallas_call(
        functools.partial(final_kernel, quarter),
        in_specs=[pl.BlockSpec(memory_space=pltpu.SMEM), vmem, vmem],
        out_shape=(
            jax.ShapeDtypeStruct((9 * C0, C1), F32),
            jax.ShapeDtypeStruct((1, C1), F32),
            jax.ShapeDtypeStruct((C1, C), F32),
        ),
        scratch_shapes=[pltpu.VMEM((4 * quarter, C1), F32)],
        compiler_params=VMEM,
        name="weight_grads",
    )(me, near, far)


def swap(value, bit, count):
    return lax.ppermute(value, "rows", [(i, i ^ bit) for i in range(count)])


def plus(a, b):
    return (a.astype(F32) + b.astype(F32)).astype(BF16)


def per_device(frames, conv_weight, conv_bias, proj_weight, target_row, target_col, cotangent):
    count = lax.axis_size("rows")
    bits = count.bit_length() - 1
    ny = count * RD
    me_word = lax.axis_index("rows").astype(jnp.int32).reshape(1)
    quarter = -(-(9 * C0 + 2 * C1 + 1) // 64) * 16

    blocks = {0: frames[1]}
    for wave in range(1, bits):
        for mask in reversed(range(2, count, 2)):
            if mask.bit_count() == wave:
                bit = mask & -mask
                blocks[mask] = swap(blocks[mask ^ bit], bit, count)
    halo = lax.ppermute(frames[0, 2 * RD - 1 :], "rows", [(i, i + 1) for i in range(count - 1)])
    grad, grad_t, wv = scatter(ny, target_row, target_col, cotangent, conv_weight)
    near = jnp.concatenate(
        [blocks[2 * reverse_bits(k, bits - 1)] for k in range(count // 2)], axis=0
    )
    near, grad, halo = lax.optimization_barrier((near, grad, halo))
    far = swap(near, 1, count)
    kept, sent, hid, first, first_grad = main(
        count, bits, quarter, me_word, near, far, frames[0], halo, wv,
        conv_bias.reshape(1, C1), proj_weight, grad, grad_t,
    )

    other = swap(sent, 1, count)
    other = plus(kept[0], other[0]), swap(plus(kept[1], other[1]), 2, count)
    lookups = lookup(ny, target_row, target_col, hid, first, proj_weight)
    total = plus(*other)
    total, lookups = lax.optimization_barrier((total, lookups))
    pixels, weights = total[: PIX * count // 4], total[PIX * count // 4 :]
    for bit in range(2, bits):
        half = pixels.shape[0] // 2
        other = swap(jnp.concatenate([pixels[half:], weights], axis=0), 1 << bit, count)
        pixels, weights = plus(pixels[:half], other[:half]), plus(weights, other[half:])
    near = jnp.stack([weights, swap(weights, 2, count)])
    tops = jnp.concatenate([first_grad, pixels], axis=0).reshape(2 * WC, RD, C1)[:, 0]
    border = lax.ppermute(tops, "rows", [(i + 1, i) for i in range(count - 1)])
    grad_input = input_grad(first_grad, pixels, border, wv)
    far = swap(near, 1, count)
    grad_conv, grad_bias, grad_proj = final(quarter, me_word, near, far)
    return lookups, grad_input, grad_conv, grad_bias.reshape(C1), grad_proj


def solution(mesh):
    split = P(None, ("pairs", "rows"))
    return jax.shard_map(
        per_device,
        mesh=mesh,
        in_specs=(P(None, ("pairs", "rows"), None), P(), P(), P(), split, split, split),
        out_specs=(
            split,
            P(None, ("pairs", "rows"), None),
            P("pairs", None),
            P("pairs"),
            P("pairs", None),
        ),
        check_vma=False,
    )
```

```python
import functools

import jax
import jax.numpy as jnp
from jax import lax
from jax.experimental import pallas as pl
from jax.experimental.pallas import tpu as pltpu
from jax.sharding import PartitionSpec as P

C = 256
C1 = 128
C0 = 96
LEVELS = 4
SPAN = 9
ITERS = 12
RD = 8
WC = 16
LOOKS = 3888
PIX = RD * WC
WIN = 384
BLOCK = PIX + 2 * WC
CHUNKS = [slice(k * LOOKS // 3, (k + 1) * LOOKS // 3) for k in range(3)]
F32 = jnp.float32
BF16 = jnp.bfloat16


def vmem_of(ny):
    return pltpu.CompilerParams(vmem_limit_bytes=(8 + ny * 3 // 16) * 1024 * 1024)

def dot(a, b):
    return jnp.dot(a, b, preferred_element_type=F32)

def dot_nt(a, b):
    return lax.dot_general(a, b, (((1,), (1,)), ((), ())), preferred_element_type=F32)

def dot_tn(a, b):
    return lax.dot_general(a, b, (((0,), (0,)), ((), ())), preferred_element_type=F32)

def iota(shape, dim):
    return lax.broadcasted_iota(jnp.int32, shape, dim)

def pick(tile, index):
    return jnp.take_along_axis(tile, index, axis=0, mode="promise_in_bounds")

def pool_matrix(ny):
    parts = []
    for level in range(1, LEVELS):
        shape = (ny >> level, ny)
        hit = iota(shape, 0) == (iota(shape, 1) >> level)
        parts.append(jnp.where(hit, 0.25**level, 0.0))
    return jnp.concatenate(parts, axis=0).astype(BF16)

def spread_matrix(ny):
    parts = []
    for level in range(1, LEVELS):
        shape = (ny, ny >> level)
        hit = (iota(shape, 0) >> level) == iota(shape, 1)
        parts.append(jnp.where(hit, 0.25**level, 0.0))
    return jnp.concatenate(parts, axis=1).astype(BF16)

def identity():
    return jnp.where(iota((C1, C1), 0) == iota((C1, C1), 1), 1.0, 0.0).astype(BF16)


def lane_row(ref, step):
    return jnp.broadcast_to(ref[pl.ds(step, 1), :], (8, PIX))

def place_columns(source, offset, cols):
    values = list(source)
    bit = 1
    while bit < cols:
        taken = (offset & bit) != 0
        last = 2 * bit >= cols
        size = len(values)
        moved = []
        for k in range(size + bit):
            if last and not 4 <= k < cols + 4:
                moved.append(None)
                continue
            here = values[k] if k < size else None
            back = values[k - bit] if 0 <= k - bit < size else None
            here = jnp.zeros((8, PIX), F32) if here is None else here
            back = jnp.zeros((8, PIX), F32) if back is None else back
            moved.append(jnp.where(taken, back, here))
        values = moved
        bit *= 2
    return values[4 : cols + 4]

def window_columns(source, offset, cols):
    zero = jnp.zeros((8, PIX), F32)
    values = [zero] * 4 + list(source) + [zero] * 4
    bit = cols // 2
    while bit >= 1:
        taken = (offset & bit) != 0
        values = [jnp.where(taken, values[k + bit], values[k]) for k in range(bit + 8)]
        bit //= 2
    return values

def scatter_kernel(
    ny, row_ref, col_ref, cot_hbm, w_ref, grad_ref, grad_t_ref, wv_ref, cot_in, cot, packed, sems, *sums
):
    sub = iota((8, PIX), 0)
    loads = [
        pltpu.make_async_copy(cot_hbm.at[part], cot_in.at[part], sems.at[k])
        for k, part in enumerate(CHUNKS)
    ]
    for load in loads:
        load.start()
    for level in range(LEVELS):
        sums[level][...] = jnp.zeros(sums[level].shape, F32)
    wv_ref[...] = jnp.zeros(wv_ref.shape, BF16)
    for tap in range(3):
        lanes = slice(tap * C1, tap * C1 + C1)
        rows = w_ref[tap * 288 : tap * 288 + 288, :]
        wv_ref[0, 32:320, lanes] = rows
        wv_ref[1, 96:384, lanes] = rows

    def step(t, carry):
        row_all, col_all = lane_row(row_ref, t), lane_row(col_ref, t)
        for level in range(LEVELS):
            cols, tiles = WC >> level, ny >> (level + 3)
            base = t * 324 + level * 81
            start = (row_all >> level) + 4
            col = col_all >> level
            shift, tile_at = start & 7, start >> 3
            body = [cot[pl.ds(base + dx, 8, stride=SPAN), :] for dx in range(SPAN)]
            tail = [
                jnp.broadcast_to(cot[pl.ds(base + 72 + dx, 1), :], (8, PIX)) for dx in range(SPAN)
            ]
            body = place_columns(body, col, cols)
            tail = place_columns(tail, col, cols)
            index = (sub - shift) & 7
            upper, lower, edge = sub >= shift, sub < shift, sub == shift
            hits = [tile_at == k for k in range(tiles + 1)]
            for v in range(cols):
                turned = pick(body[v], index)
                high = jnp.where(upper, turned, 0.0)
                low = jnp.where(lower, turned, jnp.where(edge, tail[v], 0.0))
                for k in range(tiles):
                    term = jnp.where(hits[k + 1], high, jnp.where(hits[k], low, 0.0))
                    sums[level][v, 8 * k : 8 * k + 8, :] += term
        return carry

    for k, part in enumerate(CHUNKS):
        loads[k].wait()
        cot[part, :] = cot_in[part, :].astype(F32)
        lax.fori_loop(4 * k, 4 * k + 4, step, 0)
    at = 0
    for level in range(1, LEVELS):
        for pair in range(WC // 2):
            packed[at : at + (ny >> level), pair * PIX : pair * PIX + PIX] = sums[level][
                pair >> (level - 1)
            ].astype(BF16)
        at += ny >> level
    added = dot(spread_matrix(ny), packed[...])
    for v in range(WC):
        lanes = slice(v // 2 * PIX, v // 2 * PIX + PIX)
        grad_ref[v] = (sums[0][v] + added[:, lanes]).astype(BF16)
    grad_t_ref[...] = dot_nt(identity(), grad_ref[...].reshape(WC * ny, PIX)).astype(BF16)

def scatter(ny, target_row, target_col, cotangent, conv_weight):
    vmem = pl.BlockSpec(memory_space=pltpu.VMEM)
    return pl.pallas_call(
        functools.partial(scatter_kernel, ny),
        out_shape=(
            jax.ShapeDtypeStruct((WC, ny, PIX), BF16),
            jax.ShapeDtypeStruct((PIX, WC * ny), BF16),
            jax.ShapeDtypeStruct((2, WIN, WIN), BF16),
        ),
        in_specs=[vmem, vmem, pl.BlockSpec(memory_space=pl.ANY), vmem],
        scratch_shapes=[
            pltpu.VMEM((LOOKS, PIX), BF16),
            pltpu.VMEM((LOOKS, PIX), F32),
            pltpu.VMEM((ny * 7 // 8, WC // 2 * PIX), BF16),
            pltpu.SemaphoreType.DMA((3,)),
        ]
        + [pltpu.VMEM((WC >> level, ny >> level, PIX), F32) for level in range(LEVELS)],
        compiler_params=vmem_of(ny),
        cost_estimate=pl.CostEstimate(flops=10**9, bytes_accessed=4 * 10**6, transcendentals=0),
        name="scatter",
    )(target_row, target_col, cotangent, conv_weight)

def lookup_kernel(
    ny, row_ref, col_ref, hid_ref, first_ref, proj_ref, out_hbm, looked, out, second, wide, pooled,
    sems, *volumes
):
    sub = iota((8, PIX), 0)
    first = first_ref[...]
    zero = jnp.zeros((8, PIX), F32)
    for level in range(LEVELS):
        for v in range(WC >> level):
            volumes[level][v, 0:8, :] = zero
            volumes[level][v, 8 + (ny >> level) :, :] = zero
    second[...] = dot(hid_ref[...].reshape(WC * ny, C1), proj_ref[...]).astype(BF16)
    for v in range(WC):
        wide[:, v * C : v * C + C] = second[v * ny : v * ny + ny, :]
    means = dot(pool_matrix(ny), wide[...])
    at = done = 0
    for level in range(1, LEVELS):
        size = ny >> level
        for v in range(WC >> level):
            first_at = v << level
            total = means[done : done + size, first_at * C : first_at * C + C]
            for k in range(first_at + 1, first_at + (1 << level)):
                total = total + means[done : done + size, k * C : k * C + C]
            pooled[at : at + size, :] = total.astype(BF16)
            at += size
        done += size
    scores = dot_nt(second[...], first) * (1.0 / 16.0)
    for v in range(WC):
        volumes[0][v, 8 : 8 + ny, :] = scores[v * ny : v * ny + ny]
    scores = dot_nt(pooled[...], first) * (1.0 / 16.0)
    at = 0
    for level in range(1, LEVELS):
        size = ny >> level
        for v in range(WC >> level):
            volumes[level][v, 8 : 8 + size, :] = scores[at : at + size]
            at += size

    def step(t, carry):
        row_all, col_all = lane_row(row_ref, t), lane_row(col_ref, t)
        for level in range(LEVELS):
            cols, tiles = WC >> level, ny >> (level + 3)
            base = t * 324 + level * 81
            start = (row_all >> level) + 4
            col = col_all >> level
            shift, tile_at = start & 7, start >> 3
            index = (sub + shift) & 7
            upper = sub >= shift
            beyond = tile_at >= tiles
            body, tail = [], []
            for v in range(cols):
                held = [volumes[level][v, 8 * k : 8 * k + 8, :] for k in range(tiles + 2)]
                for k in range(2):
                    held[k] = jnp.where(beyond, held[tiles + k], held[k])
                bit = tiles // 2
                while bit >= 1:
                    taken = (tile_at & bit) != 0
                    held = [jnp.where(taken, held[k + bit], held[k]) for k in range(bit + 1)]
                    bit //= 2
                body.append(pick(jnp.where(upper, held[0], held[1]), index))
                tail.append(pick(held[1], shift))
            body = window_columns(body, col, cols)
            tail = window_columns(tail, col, cols)
            for dx in range(SPAN):
                looked[pl.ds(base + dx, 8, stride=SPAN), :] = body[dx]
                looked[pl.ds(base + 72 + dx, 1), :] = tail[dx][0:1]
        return carry

    stores = []
    for k, part in enumerate(CHUNKS):
        lax.fori_loop(4 * k, 4 * k + 4, step, 0)
        out[part, :] = looked[part, :].astype(BF16)
        stores.append(pltpu.make_async_copy(out.at[part], out_hbm.at[part], sems.at[k]))
        stores[k].start()
    for store in stores:
        store.wait()

def lookup(ny, target_row, target_col, hid, first, proj_weight):
    return pl.pallas_call(
        functools.partial(lookup_kernel, ny),
        out_shape=jax.ShapeDtypeStruct((LOOKS, PIX), BF16),
        out_specs=pl.BlockSpec(memory_space=pl.ANY),
        scratch_shapes=[
            pltpu.VMEM((LOOKS, PIX), F32),
            pltpu.VMEM((LOOKS, PIX), BF16),
            pltpu.VMEM((WC * ny, C), BF16),
            pltpu.VMEM((ny, WC * C), BF16),
            pltpu.VMEM((ny * 21 // 4, C), BF16),
            pltpu.SemaphoreType.DMA((3,)),
        ]
        + [pltpu.VMEM((WC >> level, (ny >> level) + 16, PIX), F32) for level in range(LEVELS)],
        compiler_params=vmem_of(ny),
        cost_estimate=pl.CostEstimate(flops=10**9, bytes_accessed=4 * 10**6, transcendentals=0),
        name="lookup",
    )(target_row, target_col, hid, first, proj_weight)


def reverse_bits(value, bits):
    total = 0
    for bit in range(bits):
        total = total | (((value >> bit) & 1) << (bits - 1 - bit))
    return total


def row_pick(me, count, bits):
    shape = (3 * count * RD, 2 * count * RD)
    row, at = iota(shape, 0), iota(shape, 1)
    kind, row = row // (count * RD), row % (count * RD)
    line = 2 * row + jnp.where(kind == 2, -1, kind)
    place = reverse_bits(((line >> 4) & (count - 1)) ^ me, bits) * (2 * RD) + (line & 15)
    return jnp.where((place == at) & (line >= 0), 1.0, 0.0).astype(BF16)


def own_pick():
    shape = (6 * RD, 2 * RD)
    row, at = iota(shape, 0), iota(shape, 1)
    kind, row = row >> 4, row & 15
    line = 2 * row + jnp.where(kind == 2, -1, kind)
    return jnp.where((line == at) & (row < RD), 1.0, 0.0).astype(BF16)


def pixel_pick(transposed):
    a, b = iota((PIX, PIX), 0), iota((PIX, PIX), 1)
    a, b = (b, a) if transposed else (a, b)
    return jnp.where(a == (b & 7) * WC + (b >> 3), 1.0, 0.0).astype(BF16)


def main_kernel(
    count, bits, quarter, me_ref, near_ref, far_ref, own_ref, halo_ref, wv_ref, bias_ref, proj_ref,
    grad_ref, grad_t_ref, kept_ref, sent_ref, sums_kept_ref, sums_sent_ref, hid_ref, first_ref,
    first_grad_ref, views, inner, grads, rows_out, turned, pre0, below, wsum
):
    ny = count * RD
    span = 8 * ny
    me = me_ref[0]

    def place_rows(start, step, lanes_of):
        for q in range(8):
            rows = slice(start + step * q, start + step * q + step)
            after = slice(start + step * (q + 1), start + step * (q + 2))
            value = lanes_of(slice(q * WIN, q * WIN + WIN))
            for kind in range(3):
                part = value[step * kind : step * kind + step]
                views[kind, 1, rows, :] = part
                views[kind, 0, rows, 128:WIN] = part[:, 0:256]
                if q == 0:
                    views[kind, 0, rows, 0:128] = jnp.zeros((step, 128), BF16)
                if q < 7:
                    views[kind, 0, after, 0:128] = part[:, 256:WIN]

    picks = row_pick(me, count, bits)
    own_picks = own_pick()
    at_halo = iota((6 * RD, WIN), 0) == 4 * RD

    def owned(lanes):
        top = jnp.broadcast_to(halo_ref[:, lanes].astype(F32), (6 * RD, WIN))
        return jnp.where(at_halo, top, dot(own_picks, own_ref[:, lanes])).astype(BF16)

    place_rows(span, 2 * RD, owned)

    def gathered(lanes):
        rows = jnp.concatenate([near_ref[:, lanes], far_ref[:, lanes]], axis=0)
        return dot(picks, rows).astype(BF16)

    place_rows(0, ny, gathered)

    bias = bias_ref[...]
    for g in range(2):
        inner[...] = (
            dot(views[0, g], wv_ref[g, :, C1 : 2 * C1])
            + dot(views[1, g], wv_ref[g, :, 2 * C1 : 3 * C1])
            + dot(views[2, g], wv_ref[g, :, 0:C1])
            + bias
        )
        for q in range(8):
            c = 2 * q + g
            hid_ref[c] = jnp.maximum(inner[q * ny : q * ny + ny, :], 0.0).astype(BF16)
            row = span + 2 * RD * q
            pre0[8 * c : 8 * c + 8, :] = inner[row : row + 8, :]

    proj = proj_ref[...]
    hid0 = dot(pixel_pick(False), jnp.maximum(pre0[...], 0.0).astype(BF16)).astype(BF16)
    first = dot(hid0, proj).astype(BF16)
    first_ref[...] = first
    fold = (dot_nt(first, proj) * (1.0 / 16.0)).astype(BF16)
    mixed = (dot(grad_t_ref[...], hid_ref[...].reshape(WC * ny, C1)) * (1.0 / 16.0)).astype(BF16)
    grad_first = dot(mixed, proj).astype(BF16)
    grad_proj = dot_tn(mixed, first) + dot_tn(hid0, grad_first)
    pre_grad0 = dot(pixel_pick(True), dot_nt(grad_first, proj).astype(BF16))
    pre_grad0 = jnp.where(pre0[...] > 0.0, pre_grad0, 0.0)
    first_grad_ref[...] = pre_grad0.astype(BF16)
    pre0[...] = pre_grad0

    one = identity()
    bias_sum = jnp.sum(pre_grad0, axis=0, keepdims=True)
    zeros8 = jnp.zeros((8, C1), F32)
    all_grads = dot(grad_ref[...].reshape(WC * ny, PIX), fold)
    for g in range(2):
        for q in range(8):
            c = 2 * q + g
            grad = jnp.where(hid_ref[c].astype(F32) > 0.0, all_grads[c * ny : c * ny + ny], 0.0)
            bias_sum = bias_sum + jnp.sum(grad, axis=0, keepdims=True)
            grads[c, 0:ny, :] = grad
            grads[c, ny : ny + 8, :] = zeros8
            rows_out[g, q * ny : q * ny + ny, :] = grad.astype(BF16)
            own_grad = jnp.concatenate([pre_grad0[8 * c : 8 * c + 8], zeros8], axis=0)
            row = span + 2 * RD * q
            rows_out[g, row : row + 2 * RD, :] = own_grad.astype(BF16)
        turned[g] = dot_nt(one, rows_out[g]).astype(BF16)

    first_tops = pre0[pl.ds(0, WC, stride=RD), :]
    for place in range(count):
        device = reverse_bits(place, bits) ^ me
        row = pl.multiple_of(device * RD, RD)
        dest = (kept_ref, sent_ref)[place // (count // 2)]
        group = place // (count // 4) % 2
        at = BLOCK * (place % (count // 4))
        for c in range(0, WC, 2):
            dest[group, at + RD * c : at + RD * c + 2 * RD, :] = jnp.concatenate(
                [grads[c, pl.ds(row, RD), :], grads[c + 1, pl.ds(row, RD), :]], axis=0
            ).astype(BF16)
        for c in range(WC):
            below[c : c + 1, :] = grads[c, pl.ds(row + RD, 1), :]
        dest[group, at + PIX : at + PIX + WC, :] = below[...].astype(BF16)
        dest[group, at + PIX + WC : at + BLOCK, :] = jnp.where(
            device + 1 == me, first_tops, 0.0
        ).astype(BF16)

    parts = [[dot(turned[g], views[kind, g]) for g in range(2)] for kind in range(3)]
    wsum[9 * C0 + 2 * C1 :, :] = jnp.zeros((4 * quarter - 9 * C0 - 2 * C1, C1), F32)
    for tap in range(3):
        left, right = parts[(tap - 1) % 3]
        wsum[tap * 288 : tap * 288 + 288, :] = left.T[32:320] + right.T[96:384]
    wsum[9 * C0 : 9 * C0 + C1, :] = grad_proj[:, 0:C1]
    wsum[9 * C0 + C1 : 9 * C0 + 2 * C1, :] = grad_proj[:, C1:]
    wsum[9 * C0 + 2 * C1 : 9 * C0 + 2 * C1 + 1, :] = bias_sum
    for place in range(4):
        row = pl.multiple_of((place ^ reverse_bits(me & 3, 2)) * quarter, 16)
        dest = (sums_kept_ref, sums_sent_ref)[place // 2]
        dest[place % 2] = wsum[pl.ds(row, quarter), :].astype(BF16)


def main(count, bits, quarter, me, near, far, own, halo, wv, bias, proj_weight, grad, grad_t):
    ny = count * RD
    rows = 8 * ny + PIX
    vmem = pl.BlockSpec(memory_space=pltpu.VMEM)
    pixels, sums = (2, BLOCK * count // 4, C1), (2, quarter, C1)
    return pl.pallas_call(
        functools.partial(main_kernel, count, bits, quarter),
        in_specs=[pl.BlockSpec(memory_space=pltpu.SMEM)] + [vmem] * 9,
        out_shape=(
            jax.ShapeDtypeStruct(pixels, BF16),
            jax.ShapeDtypeStruct(pixels, BF16),
            jax.ShapeDtypeStruct(sums, BF16),
            jax.ShapeDtypeStruct(sums, BF16),
            jax.ShapeDtypeStruct((WC, ny, C1), BF16),
            jax.ShapeDtypeStruct((PIX, C), BF16),
            jax.ShapeDtypeStruct((PIX, C1), BF16),
        ),
        scratch_shapes=[
            pltpu.VMEM((3, 2, rows, WIN), BF16),
            pltpu.VMEM((rows, C1), F32),
            pltpu.VMEM((WC, ny + 8, C1), F32),
            pltpu.VMEM((2, rows, C1), BF16),
            pltpu.VMEM((2, C1, rows), BF16),
            pltpu.VMEM((PIX, C1), F32),
            pltpu.VMEM((WC, C1), F32),
            pltpu.VMEM((4 * quarter, C1), F32),
        ],
        compiler_params=vmem_of(ny),
        cost_estimate=pl.CostEstimate(flops=4 * 10**9, bytes_accessed=6 * 10**6, transcendentals=0),
        name="features",
    )(me, near, far, own, halo, wv, bias, proj_weight, grad, grad_t)


def input_kernel(first_ref, block_ref, wv_ref, out_ref, sides, full):
    last = iota((8, C1), 0) == 7
    grads = [first_ref[...].astype(F32), block_ref[0:PIX, :].astype(F32)]
    border = block_ref[PIX:, :].astype(F32)

    def spread(g):
        here, both = [], []
        for c in range(g, WC, 2):
            for f in range(2):
                own = grads[f][8 * c : 8 * c + 8]
                at = WC * (1 - f) + c
                below = jnp.broadcast_to(border[at : at + 1], (8, C1))
                here.append(own)
                both.append(
                    jnp.concatenate([own, jnp.where(last, below, pltpu.roll(own, 7, 0))], axis=1)
                )
        here = jnp.concatenate(here, axis=0).astype(BF16)
        both = jnp.concatenate(both, axis=0).astype(BF16)
        weights = wv_ref[g]
        outer = jnp.concatenate([weights[:, 2 * C1 : 3 * C1], weights[:, 0:C1]], axis=1)
        return dot_nt(here, weights[:, C1 : 2 * C1]), dot_nt(both, outer)

    even, odd = spread(0), spread(1)
    for parity in range(2):
        for q in range(8):
            sides[parity, :, q * WIN : q * WIN + WIN] = odd[parity][16 * q : 16 * q + 16]
        sides[parity, :, 0:256] += even[parity][0:16, 128:WIN]
        for q in range(1, 8):
            sides[parity, :, q * WIN - 128 : q * WIN + 256] += even[parity][16 * q : 16 * q + 16]
        for f in range(2):
            for j in range(2 * WC * C0 // 128):
                lanes = slice(128 * j, 128 * j + 128)
                full[f, j, pl.ds(parity, 8, stride=2), :] = sides[parity, 8 * f : 8 * f + 8, lanes]
    for f in range(2):
        for j in range(2 * WC * C0 // 128):
            out_ref[f, :, 128 * j : 128 * j + 128] = full[f, j].astype(BF16)


def input_grad(first_grad, block, wv):
    return pl.pallas_call(
        input_kernel,
        out_shape=jax.ShapeDtypeStruct((2, 2 * RD, 2 * WC * C0), BF16),
        scratch_shapes=[
            pltpu.VMEM((2, 2 * RD, 2 * WC * C0), F32),
            pltpu.VMEM((2, 2 * WC * C0 // 128, 2 * RD, 128), F32),
        ],
        compiler_params=vmem_of(0),
        cost_estimate=pl.CostEstimate(flops=10**8, bytes_accessed=10**6, transcendentals=0),
        name="input_grad",
    )(first_grad, block, wv)


def final_kernel(quarter, me_ref, near_ref, far_ref, conv_ref, bias_ref, proj_ref, wsum):
    turned = reverse_bits(me_ref[0] & 3, 2)
    for place in range(4):
        ref = (near_ref, far_ref)[place // 2]
        row = pl.multiple_of((place ^ turned) * quarter, 16)
        wsum[pl.ds(row, quarter), :] = ref[place % 2].astype(F32)
    conv_ref[...] = wsum[0 : 9 * C0, :]
    proj_ref[:, 0:C1] = wsum[9 * C0 : 9 * C0 + C1, :]
    proj_ref[:, C1:] = wsum[9 * C0 + C1 : 9 * C0 + 2 * C1, :]
    bias_ref[...] = wsum[9 * C0 + 2 * C1 : 9 * C0 + 2 * C1 + 1, :]


def final(quarter, me, near, far):
    vmem = pl.BlockSpec(memory_space=pltpu.VMEM)
    return pl.pallas_call(
        functools.partial(final_kernel, quarter),
        in_specs=[pl.BlockSpec(memory_space=pltpu.SMEM), vmem, vmem],
        out_shape=(
            jax.ShapeDtypeStruct((9 * C0, C1), F32),
            jax.ShapeDtypeStruct((1, C1), F32),
            jax.ShapeDtypeStruct((C1, C), F32),
        ),
        scratch_shapes=[pltpu.VMEM((4 * quarter, C1), F32)],
        compiler_params=vmem_of(0),
        name="weight_grads",
    )(me, near, far)


def swap(value, bit, count):
    return lax.ppermute(value, "rows", [(i, i ^ bit) for i in range(count)])


def plus(a, b):
    return (a.astype(F32) + b.astype(F32)).astype(BF16)


def per_device(frames, conv_weight, conv_bias, proj_weight, target_row, target_col, cotangent):
    count = lax.axis_size("rows")
    bits = count.bit_length() - 1
    ny = count * RD
    me_word = lax.axis_index("rows").astype(jnp.int32).reshape(1)
    quarter = -(-(9 * C0 + 2 * C1 + 1) // 64) * 16

    blocks = {0: frames[1]}
    for wave in range(1, bits):
        for mask in reversed(range(2, count, 2)):
            if mask.bit_count() == wave and mask != count - 2:
                bit = mask & -mask
                blocks[mask] = swap(blocks[mask ^ bit], bit, count)
    halo = lax.ppermute(frames[0, 2 * RD - 1 :], "rows", [(i, i + 1) for i in range(count - 1)])
    last = blocks[count - 4]
    target_row, target_col, cotangent, last = lax.optimization_barrier(
        (target_row, target_col, cotangent, last)
    )
    blocks[count - 4] = last
    blocks[count - 2] = swap(last, 2, count)
    grad, grad_t, wv = scatter(ny, target_row, target_col, cotangent, conv_weight)
    near = jnp.concatenate(
        [blocks[2 * reverse_bits(k, bits - 1)] for k in range(count // 2)], axis=0
    )
    near, grad, halo = lax.optimization_barrier((near, grad, halo))
    far = swap(near, 1, count)
    kept, sent, sums_kept, sums_sent, hid, first, first_grad = main(
        count, bits, quarter, me_word, near, far, frames[0], halo, wv,
        conv_bias.reshape(1, C1), proj_weight, grad, grad_t,
    )

    other_sums = swap(sums_sent, 1, count)
    other = swap(sent, 1, count)
    arrived = swap(plus(sums_kept[1], other_sums[1]), 2, count)
    sums = plus(plus(sums_kept[0], other_sums[0]), arrived)
    given = plus(kept[1], other[1])
    pixels = plus(kept[0], other[0])
    given, sums, pixels = lax.optimization_barrier((given, sums, pixels))
    arrived = swap(sums, 4, count)
    pixels_arrived = swap(given, 2, count)
    sums = plus(sums, arrived)
    arrived = None
    lookups = lookup(ny, target_row, target_col, hid, first, proj_weight)
    for bit in range(3, bits):
        sums = plus(sums, swap(sums, 1 << bit, count))
    sums, lookups = lax.optimization_barrier((sums, lookups))
    pixels = plus(pixels, pixels_arrived)
    near = jnp.stack([sums, swap(sums, 2, count)])
    for bit in range(2, bits):
        half = pixels.shape[0] // 2
        other = swap(pixels[half:], 1 << bit, count)
        pixels = plus(pixels[:half], other)
    far = swap(near, 1, count)
    grad_input = input_grad(first_grad, pixels, wv)
    grad_conv, grad_bias, grad_proj = final(quarter, me_word, near, far)
    return lookups, grad_input, grad_conv, grad_bias.reshape(C1), grad_proj


def solution(mesh):
    split = P(None, ("pairs", "rows"))
    return jax.shard_map(
        per_device,
        mesh=mesh,
        in_specs=(P(None, ("pairs", "rows"), None), P(), P(), P(), split, split, split),
        out_specs=(
            split,
            P(None, ("pairs", "rows"), None),
            P("pairs", None),
            P("pairs"),
            P("pairs", None),
        ),
        check_vma=False,
    )
```

```python
import functools

import jax
import jax.numpy as jnp
from jax import lax
from jax.experimental import pallas as pl
from jax.experimental.pallas import tpu as pltpu
from jax.sharding import PartitionSpec as P

C = 256
C1 = 128
C0 = 96
LEVELS = 4
SPAN = 9
ITERS = 12
RD = 8
WC = 16
LOOKS = 3888
PIX = RD * WC
WIN = 384
BLOCK = PIX + 2 * WC
CHUNKS = [slice(k * LOOKS // 3, (k + 1) * LOOKS // 3) for k in range(3)]
F32 = jnp.float32
BF16 = jnp.bfloat16


def vmem_of(ny):
    return pltpu.CompilerParams(vmem_limit_bytes=(8 + ny * 3 // 16) * 1024 * 1024)

def dot(a, b):
    return jnp.dot(a, b, preferred_element_type=F32)

def dot_nt(a, b):
    return lax.dot_general(a, b, (((1,), (1,)), ((), ())), preferred_element_type=F32)

def dot_tn(a, b):
    return lax.dot_general(a, b, (((0,), (0,)), ((), ())), preferred_element_type=F32)

def iota(shape, dim):
    return lax.broadcasted_iota(jnp.int32, shape, dim)

def pick(tile, index):
    return jnp.take_along_axis(tile, index, axis=0, mode="promise_in_bounds")

def pool_matrix(ny):
    parts = []
    for level in range(1, LEVELS):
        shape = (ny >> level, ny)
        hit = iota(shape, 0) == (iota(shape, 1) >> level)
        parts.append(jnp.where(hit, 0.25**level, 0.0))
    return jnp.concatenate(parts, axis=0).astype(BF16)

def spread_matrix(ny):
    parts = []
    for level in range(1, LEVELS):
        shape = (ny, ny >> level)
        hit = (iota(shape, 0) >> level) == iota(shape, 1)
        parts.append(jnp.where(hit, 0.25**level, 0.0))
    return jnp.concatenate(parts, axis=1).astype(BF16)

def identity():
    return jnp.where(iota((C1, C1), 0) == iota((C1, C1), 1), 1.0, 0.0).astype(BF16)


def lane_row(ref, step):
    return jnp.broadcast_to(ref[pl.ds(step, 1), :], (8, PIX))

def place_columns(source, offset, cols):
    values = list(source)
    bit = 1
    while bit < cols:
        taken = (offset & bit) != 0
        last = 2 * bit >= cols
        size = len(values)
        moved = []
        for k in range(size + bit):
            if last and not 4 <= k < cols + 4:
                moved.append(None)
                continue
            here = values[k] if k < size else None
            back = values[k - bit] if 0 <= k - bit < size else None
            here = jnp.zeros((8, PIX), F32) if here is None else here
            back = jnp.zeros((8, PIX), F32) if back is None else back
            moved.append(jnp.where(taken, back, here))
        values = moved
        bit *= 2
    return values[4 : cols + 4]

def window_columns(source, offset, cols):
    zero = jnp.zeros((8, PIX), F32)
    values = [zero] * 4 + list(source) + [zero] * 4
    bit = cols // 2
    while bit >= 1:
        taken = (offset & bit) != 0
        values = [jnp.where(taken, values[k + bit], values[k]) for k in range(bit + 8)]
        bit //= 2
    return values

def scatter_kernel(
    ny, row_ref, col_ref, cot_hbm, grad_ref, grad_t_ref, cot_in, cot, packed, sems, *sums
):
    sub = iota((8, PIX), 0)
    loads = [
        pltpu.make_async_copy(cot_hbm.at[part], cot_in.at[part], sems.at[k])
        for k, part in enumerate(CHUNKS)
    ]
    for load in loads:
        load.start()
    for level in range(LEVELS):
        sums[level][...] = jnp.zeros(sums[level].shape, F32)
    def step(t, carry):
        row_all, col_all = lane_row(row_ref, t), lane_row(col_ref, t)
        for level in range(LEVELS):
            cols, tiles = WC >> level, ny >> (level + 3)
            base = t * 324 + level * 81
            start = (row_all >> level) + 4
            col = col_all >> level
            shift, tile_at = start & 7, start >> 3
            body = [cot[pl.ds(base + dx, 8, stride=SPAN), :] for dx in range(SPAN)]
            tail = [
                jnp.broadcast_to(cot[pl.ds(base + 72 + dx, 1), :], (8, PIX)) for dx in range(SPAN)
            ]
            body = place_columns(body, col, cols)
            tail = place_columns(tail, col, cols)
            index = (sub - shift) & 7
            upper, lower, edge = sub >= shift, sub < shift, sub == shift
            hits = [tile_at == k for k in range(tiles + 1)]
            for v in range(cols):
                turned = pick(body[v], index)
                high = jnp.where(upper, turned, 0.0)
                low = jnp.where(lower, turned, jnp.where(edge, tail[v], 0.0))
                for k in range(tiles):
                    term = jnp.where(hits[k + 1], high, jnp.where(hits[k], low, 0.0))
                    sums[level][v, 8 * k : 8 * k + 8, :] += term
        return carry

    for k, part in enumerate(CHUNKS):
        loads[k].wait()
        cot[part, :] = cot_in[part, :].astype(F32)
        lax.fori_loop(4 * k, 4 * k + 4, step, 0)
    at = 0
    for level in range(1, LEVELS):
        for pair in range(WC // 2):
            packed[at : at + (ny >> level), pair * PIX : pair * PIX + PIX] = sums[level][
                pair >> (level - 1)
            ].astype(BF16)
        at += ny >> level
    added = dot(spread_matrix(ny), packed[...])
    for v in range(WC):
        lanes = slice(v // 2 * PIX, v // 2 * PIX + PIX)
        grad_ref[v] = (sums[0][v] + added[:, lanes]).astype(BF16)
    grad_t_ref[...] = dot_nt(identity(), grad_ref[...].reshape(WC * ny, PIX)).astype(BF16)

def scatter(ny, target_row, target_col, cotangent):
    vmem = pl.BlockSpec(memory_space=pltpu.VMEM)
    return pl.pallas_call(
        functools.partial(scatter_kernel, ny),
        out_shape=(
            jax.ShapeDtypeStruct((WC, ny, PIX), BF16),
            jax.ShapeDtypeStruct((PIX, WC * ny), BF16),
        ),
        in_specs=[vmem, vmem, pl.BlockSpec(memory_space=pl.ANY)],
        scratch_shapes=[
            pltpu.VMEM((LOOKS, PIX), BF16),
            pltpu.VMEM((LOOKS, PIX), F32),
            pltpu.VMEM((ny * 7 // 8, WC // 2 * PIX), BF16),
            pltpu.SemaphoreType.DMA((3,)),
        ]
        + [pltpu.VMEM((WC >> level, ny >> level, PIX), F32) for level in range(LEVELS)],
        compiler_params=vmem_of(ny),
        cost_estimate=pl.CostEstimate(flops=10**9, bytes_accessed=4 * 10**6, transcendentals=0),
        name="scatter",
    )(target_row, target_col, cotangent)

def prepare_kernel(row_ref, col_ref, w_ref, bias_ref, proj_ref, row_out, col_out, wv_ref, bias_out, proj_out):
    row_out[...] = row_ref[...]
    col_out[...] = col_ref[...]
    bias_out[...] = bias_ref[...]
    proj_out[...] = proj_ref[...]
    wv_ref[...] = jnp.zeros(wv_ref.shape, BF16)
    for tap in range(3):
        lanes = slice(tap * C1, tap * C1 + C1)
        rows = w_ref[tap * 288 : tap * 288 + 288, :]
        wv_ref[0, 32:320, lanes] = rows
        wv_ref[1, 96:384, lanes] = rows


def prepare(target_row, target_col, conv_weight, conv_bias, proj_weight):
    same = [jax.ShapeDtypeStruct(a.shape, a.dtype) for a in (target_row, conv_bias, proj_weight)]
    return pl.pallas_call(
        prepare_kernel,
        out_shape=(
            same[0], same[0], jax.ShapeDtypeStruct((2, WIN, WIN), BF16), same[1], same[2]
        ),
        compiler_params=vmem_of(0),
        cost_estimate=pl.CostEstimate(flops=10**6, bytes_accessed=10**6, transcendentals=0),
        name="prepare",
    )(target_row, target_col, conv_weight, conv_bias, proj_weight)


def lookup_kernel(
    ny, row_ref, col_ref, hid_ref, first_ref, proj_ref, out_hbm, looked, out, second, wide, pooled,
    sems, *volumes
):
    sub = iota((8, PIX), 0)
    first = first_ref[...]
    zero = jnp.zeros((8, PIX), F32)
    for level in range(LEVELS):
        for v in range(WC >> level):
            volumes[level][v, 0:8, :] = zero
            volumes[level][v, 8 + (ny >> level) :, :] = zero
    second[...] = dot(hid_ref[...].reshape(WC * ny, C1), proj_ref[...]).astype(BF16)
    for v in range(WC):
        wide[:, v * C : v * C + C] = second[v * ny : v * ny + ny, :]
    means = dot(pool_matrix(ny), wide[...])
    at = done = 0
    for level in range(1, LEVELS):
        size = ny >> level
        for v in range(WC >> level):
            first_at = v << level
            total = means[done : done + size, first_at * C : first_at * C + C]
            for k in range(first_at + 1, first_at + (1 << level)):
                total = total + means[done : done + size, k * C : k * C + C]
            pooled[at : at + size, :] = total.astype(BF16)
            at += size
        done += size
    scores = dot_nt(second[...], first) * (1.0 / 16.0)
    for v in range(WC):
        volumes[0][v, 8 : 8 + ny, :] = scores[v * ny : v * ny + ny]
    scores = dot_nt(pooled[...], first) * (1.0 / 16.0)
    at = 0
    for level in range(1, LEVELS):
        size = ny >> level
        for v in range(WC >> level):
            volumes[level][v, 8 : 8 + size, :] = scores[at : at + size]
            at += size

    def step(t, carry):
        row_all, col_all = lane_row(row_ref, t), lane_row(col_ref, t)
        for level in range(LEVELS):
            cols, tiles = WC >> level, ny >> (level + 3)
            base = t * 324 + level * 81
            start = (row_all >> level) + 4
            col = col_all >> level
            shift, tile_at = start & 7, start >> 3
            index = (sub + shift) & 7
            upper = sub >= shift
            beyond = tile_at >= tiles
            body, tail = [], []
            for v in range(cols):
                held = [volumes[level][v, 8 * k : 8 * k + 8, :] for k in range(tiles + 2)]
                for k in range(2):
                    held[k] = jnp.where(beyond, held[tiles + k], held[k])
                bit = tiles // 2
                while bit >= 1:
                    taken = (tile_at & bit) != 0
                    held = [jnp.where(taken, held[k + bit], held[k]) for k in range(bit + 1)]
                    bit //= 2
                body.append(pick(jnp.where(upper, held[0], held[1]), index))
                tail.append(pick(held[1], shift))
            body = window_columns(body, col, cols)
            tail = window_columns(tail, col, cols)
            for dx in range(SPAN):
                looked[pl.ds(base + dx, 8, stride=SPAN), :] = body[dx]
                looked[pl.ds(base + 72 + dx, 1), :] = tail[dx][0:1]
        return carry

    stores = []
    for k, part in enumerate(CHUNKS):
        lax.fori_loop(4 * k, 4 * k + 4, step, 0)
        out[part, :] = looked[part, :].astype(BF16)
        stores.append(pltpu.make_async_copy(out.at[part], out_hbm.at[part], sems.at[k]))
        stores[k].start()
    for store in stores:
        store.wait()

def lookup(ny, target_row, target_col, hid, first, proj_weight):
    return pl.pallas_call(
        functools.partial(lookup_kernel, ny),
        out_shape=jax.ShapeDtypeStruct((LOOKS, PIX), BF16),
        out_specs=pl.BlockSpec(memory_space=pl.ANY),
        scratch_shapes=[
            pltpu.VMEM((LOOKS, PIX), F32),
            pltpu.VMEM((LOOKS, PIX), BF16),
            pltpu.VMEM((WC * ny, C), BF16),
            pltpu.VMEM((ny, WC * C), BF16),
            pltpu.VMEM((ny * 21 // 4, C), BF16),
            pltpu.SemaphoreType.DMA((3,)),
        ]
        + [pltpu.VMEM((WC >> level, (ny >> level) + 16, PIX), F32) for level in range(LEVELS)],
        compiler_params=vmem_of(ny),
        cost_estimate=pl.CostEstimate(flops=10**9, bytes_accessed=4 * 10**6, transcendentals=0),
        name="lookup",
    )(target_row, target_col, hid, first, proj_weight)


def reverse_bits(value, bits):
    total = 0
    for bit in range(bits):
        total = total | (((value >> bit) & 1) << (bits - 1 - bit))
    return total


def row_pick(me, count, bits):
    shape = (3 * count * RD, 2 * count * RD)
    row, at = iota(shape, 0), iota(shape, 1)
    kind, row = row // (count * RD), row % (count * RD)
    line = 2 * row + jnp.where(kind == 2, -1, kind)
    place = reverse_bits(((line >> 4) & (count - 1)) ^ me, bits) * (2 * RD) + (line & 15)
    return jnp.where((place == at) & (line >= 0), 1.0, 0.0).astype(BF16)


def own_pick():
    shape = (6 * RD, 2 * RD)
    row, at = iota(shape, 0), iota(shape, 1)
    kind, row = row >> 4, row & 15
    line = 2 * row + jnp.where(kind == 2, -1, kind)
    return jnp.where((line == at) & (row < RD), 1.0, 0.0).astype(BF16)


def pixel_pick(transposed):
    a, b = iota((PIX, PIX), 0), iota((PIX, PIX), 1)
    a, b = (b, a) if transposed else (a, b)
    return jnp.where(a == (b & 7) * WC + (b >> 3), 1.0, 0.0).astype(BF16)


def main_kernel(
    count, bits, quarter, me_ref, near_ref, far_ref, own_ref, halo_ref, wv_ref, bias_ref, proj_ref,
    grad_ref, grad_t_ref, kept_ref, sent_ref, sums_kept_ref, sums_sent_ref, hid_ref, first_ref,
    first_grad_ref, views, inner, grads, rows_out, turned, pre0, below, wsum
):
    ny = count * RD
    span = 8 * ny
    me = me_ref[0]

    def place_rows(start, step, lanes_of):
        for q in range(8):
            rows = slice(start + step * q, start + step * q + step)
            after = slice(start + step * (q + 1), start + step * (q + 2))
            value = lanes_of(slice(q * WIN, q * WIN + WIN))
            for kind in range(3):
                part = value[step * kind : step * kind + step]
                views[kind, 1, rows, :] = part
                views[kind, 0, rows, 128:WIN] = part[:, 0:256]
                if q == 0:
                    views[kind, 0, rows, 0:128] = jnp.zeros((step, 128), BF16)
                if q < 7:
                    views[kind, 0, after, 0:128] = part[:, 256:WIN]

    picks = row_pick(me, count, bits)
    own_picks = own_pick()
    at_halo = iota((6 * RD, WIN), 0) == 4 * RD

    def owned(lanes):
        top = jnp.broadcast_to(halo_ref[:, lanes].astype(F32), (6 * RD, WIN))
        return jnp.where(at_halo, top, dot(own_picks, own_ref[:, lanes])).astype(BF16)

    place_rows(span, 2 * RD, owned)

    def gathered(lanes):
        rows = jnp.concatenate([near_ref[:, lanes], far_ref[:, lanes]], axis=0)
        return dot(picks, rows).astype(BF16)

    place_rows(0, ny, gathered)

    bias = bias_ref[...]
    for g in range(2):
        inner[...] = (
            dot(views[0, g], wv_ref[g, :, C1 : 2 * C1])
            + dot(views[1, g], wv_ref[g, :, 2 * C1 : 3 * C1])
            + dot(views[2, g], wv_ref[g, :, 0:C1])
            + bias
        )
        for q in range(8):
            c = 2 * q + g
            hid_ref[c] = jnp.maximum(inner[q * ny : q * ny + ny, :], 0.0).astype(BF16)
            row = span + 2 * RD * q
            pre0[8 * c : 8 * c + 8, :] = inner[row : row + 8, :]

    proj = proj_ref[...]
    hid0 = dot(pixel_pick(False), jnp.maximum(pre0[...], 0.0).astype(BF16)).astype(BF16)
    first = dot(hid0, proj).astype(BF16)
    first_ref[...] = first
    fold = (dot_nt(first, proj) * (1.0 / 16.0)).astype(BF16)
    mixed = (dot(grad_t_ref[...], hid_ref[...].reshape(WC * ny, C1)) * (1.0 / 16.0)).astype(BF16)
    grad_first = dot(mixed, proj).astype(BF16)
    grad_proj = dot_tn(mixed, first) + dot_tn(hid0, grad_first)
    pre_grad0 = dot(pixel_pick(True), dot_nt(grad_first, proj).astype(BF16))
    pre_grad0 = jnp.where(pre0[...] > 0.0, pre_grad0, 0.0)
    first_grad_ref[...] = pre_grad0.astype(BF16)
    pre0[...] = pre_grad0

    one = identity()
    bias_sum = jnp.sum(pre_grad0, axis=0, keepdims=True)
    zeros8 = jnp.zeros((8, C1), F32)
    all_grads = dot(grad_ref[...].reshape(WC * ny, PIX), fold)
    for g in range(2):
        for q in range(8):
            c = 2 * q + g
            grad = jnp.where(hid_ref[c].astype(F32) > 0.0, all_grads[c * ny : c * ny + ny], 0.0)
            bias_sum = bias_sum + jnp.sum(grad, axis=0, keepdims=True)
            grads[c, 0:ny, :] = grad
            grads[c, ny : ny + 8, :] = zeros8
            rows_out[g, q * ny : q * ny + ny, :] = grad.astype(BF16)
            own_grad = jnp.concatenate([pre_grad0[8 * c : 8 * c + 8], zeros8], axis=0)
            row = span + 2 * RD * q
            rows_out[g, row : row + 2 * RD, :] = own_grad.astype(BF16)
        turned[g] = dot_nt(one, rows_out[g]).astype(BF16)

    first_tops = pre0[pl.ds(0, WC, stride=RD), :]
    for place in range(count):
        device = reverse_bits(place, bits) ^ me
        row = pl.multiple_of(device * RD, RD)
        dest = (kept_ref, sent_ref)[place // (count // 2)]
        group = place // (count // 4) % 2
        at = BLOCK * (place % (count // 4))
        for c in range(0, WC, 2):
            dest[group, at + RD * c : at + RD * c + 2 * RD, :] = jnp.concatenate(
                [grads[c, pl.ds(row, RD), :], grads[c + 1, pl.ds(row, RD), :]], axis=0
            ).astype(BF16)
        for c in range(WC):
            below[c : c + 1, :] = grads[c, pl.ds(row + RD, 1), :]
        dest[group, at + PIX : at + PIX + WC, :] = below[...].astype(BF16)
        dest[group, at + PIX + WC : at + BLOCK, :] = jnp.where(
            device + 1 == me, first_tops, 0.0
        ).astype(BF16)

    parts = [[dot(turned[g], views[kind, g]) for g in range(2)] for kind in range(3)]
    wsum[9 * C0 + 2 * C1 :, :] = jnp.zeros((4 * quarter - 9 * C0 - 2 * C1, C1), F32)
    for tap in range(3):
        left, right = parts[(tap - 1) % 3]
        wsum[tap * 288 : tap * 288 + 288, :] = left.T[32:320] + right.T[96:384]
    wsum[9 * C0 : 9 * C0 + C1, :] = grad_proj[:, 0:C1]
    wsum[9 * C0 + C1 : 9 * C0 + 2 * C1, :] = grad_proj[:, C1:]
    wsum[9 * C0 + 2 * C1 : 9 * C0 + 2 * C1 + 1, :] = bias_sum
    for place in range(4):
        row = pl.multiple_of((place ^ reverse_bits(me & 3, 2)) * quarter, 16)
        dest = (sums_kept_ref, sums_sent_ref)[place // 2]
        dest[place % 2] = wsum[pl.ds(row, quarter), :].astype(BF16)


def main(count, bits, quarter, me, near, far, own, halo, wv, bias, proj_weight, grad, grad_t):
    ny = count * RD
    rows = 8 * ny + PIX
    vmem = pl.BlockSpec(memory_space=pltpu.VMEM)
    pixels, sums = (2, BLOCK * count // 4, C1), (2, quarter, C1)
    return pl.pallas_call(
        functools.partial(main_kernel, count, bits, quarter),
        in_specs=[pl.BlockSpec(memory_space=pltpu.SMEM)] + [vmem] * 9,
        out_shape=(
            jax.ShapeDtypeStruct(pixels, BF16),
            jax.ShapeDtypeStruct(pixels, BF16),
            jax.ShapeDtypeStruct(sums, BF16),
            jax.ShapeDtypeStruct(sums, BF16),
            jax.ShapeDtypeStruct((WC, ny, C1), BF16),
            jax.ShapeDtypeStruct((PIX, C), BF16),
            jax.ShapeDtypeStruct((PIX, C1), BF16),
        ),
        scratch_shapes=[
            pltpu.VMEM((3, 2, rows, WIN), BF16),
            pltpu.VMEM((rows, C1), F32),
            pltpu.VMEM((WC, ny + 8, C1), F32),
            pltpu.VMEM((2, rows, C1), BF16),
            pltpu.VMEM((2, C1, rows), BF16),
            pltpu.VMEM((PIX, C1), F32),
            pltpu.VMEM((WC, C1), F32),
            pltpu.VMEM((4 * quarter, C1), F32),
        ],
        compiler_params=vmem_of(ny),
        cost_estimate=pl.CostEstimate(flops=4 * 10**9, bytes_accessed=6 * 10**6, transcendentals=0),
        name="features",
    )(me, near, far, own, halo, wv, bias, proj_weight, grad, grad_t)


def input_kernel(first_ref, block_ref, wv_ref, out_ref, sides, full):
    last = iota((8, C1), 0) == 7
    grads = [first_ref[...].astype(F32), block_ref[0:PIX, :].astype(F32)]
    border = block_ref[PIX:, :].astype(F32)

    def spread(g):
        here, both = [], []
        for c in range(g, WC, 2):
            for f in range(2):
                own = grads[f][8 * c : 8 * c + 8]
                at = WC * (1 - f) + c
                below = jnp.broadcast_to(border[at : at + 1], (8, C1))
                here.append(own)
                both.append(
                    jnp.concatenate([own, jnp.where(last, below, pltpu.roll(own, 7, 0))], axis=1)
                )
        here = jnp.concatenate(here, axis=0).astype(BF16)
        both = jnp.concatenate(both, axis=0).astype(BF16)
        weights = wv_ref[g]
        outer = jnp.concatenate([weights[:, 2 * C1 : 3 * C1], weights[:, 0:C1]], axis=1)
        return dot_nt(here, weights[:, C1 : 2 * C1]), dot_nt(both, outer)

    even, odd = spread(0), spread(1)
    for parity in range(2):
        for q in range(8):
            sides[parity, :, q * WIN : q * WIN + WIN] = odd[parity][16 * q : 16 * q + 16]
        sides[parity, :, 0:256] += even[parity][0:16, 128:WIN]
        for q in range(1, 8):
            sides[parity, :, q * WIN - 128 : q * WIN + 256] += even[parity][16 * q : 16 * q + 16]
        for f in range(2):
            for j in range(2 * WC * C0 // 128):
                lanes = slice(128 * j, 128 * j + 128)
                full[f, j, pl.ds(parity, 8, stride=2), :] = sides[parity, 8 * f : 8 * f + 8, lanes]
    for f in range(2):
        for j in range(2 * WC * C0 // 128):
            out_ref[f, :, 128 * j : 128 * j + 128] = full[f, j].astype(BF16)


def input_grad(first_grad, block, wv):
    return pl.pallas_call(
        input_kernel,
        out_shape=jax.ShapeDtypeStruct((2, 2 * RD, 2 * WC * C0), BF16),
        scratch_shapes=[
            pltpu.VMEM((2, 2 * RD, 2 * WC * C0), F32),
            pltpu.VMEM((2, 2 * WC * C0 // 128, 2 * RD, 128), F32),
        ],
        compiler_params=vmem_of(0),
        cost_estimate=pl.CostEstimate(flops=10**8, bytes_accessed=10**6, transcendentals=0),
        name="input_grad",
    )(first_grad, block, wv)


def final_kernel(quarter, me_ref, near_ref, far_ref, conv_ref, bias_ref, proj_ref, wsum):
    turned = reverse_bits(me_ref[0] & 3, 2)
    for place in range(4):
        ref = (near_ref, far_ref)[place // 2]
        row = pl.multiple_of((place ^ turned) * quarter, 16)
        wsum[pl.ds(row, quarter), :] = ref[place % 2].astype(F32)
    conv_ref[...] = wsum[0 : 9 * C0, :]
    proj_ref[:, 0:C1] = wsum[9 * C0 : 9 * C0 + C1, :]
    proj_ref[:, C1:] = wsum[9 * C0 + C1 : 9 * C0 + 2 * C1, :]
    bias_ref[...] = wsum[9 * C0 + 2 * C1 : 9 * C0 + 2 * C1 + 1, :]


def final(quarter, me, near, far):
    vmem = pl.BlockSpec(memory_space=pltpu.VMEM)
    return pl.pallas_call(
        functools.partial(final_kernel, quarter),
        in_specs=[pl.BlockSpec(memory_space=pltpu.SMEM), vmem, vmem],
        out_shape=(
            jax.ShapeDtypeStruct((9 * C0, C1), F32),
            jax.ShapeDtypeStruct((1, C1), F32),
            jax.ShapeDtypeStruct((C1, C), F32),
        ),
        scratch_shapes=[pltpu.VMEM((4 * quarter, C1), F32)],
        compiler_params=vmem_of(0),
        name="weight_grads",
    )(me, near, far)


def swap(value, bit, count):
    return lax.ppermute(value, "rows", [(i, i ^ bit) for i in range(count)])


def plus(a, b):
    return (a.astype(F32) + b.astype(F32)).astype(BF16)


def per_device(frames, conv_weight, conv_bias, proj_weight, target_row, target_col, cotangent):
    count = lax.axis_size("rows")
    bits = count.bit_length() - 1
    ny = count * RD
    me_word = lax.axis_index("rows").astype(jnp.int32).reshape(1)
    quarter = -(-(9 * C0 + 2 * C1 + 1) // 64) * 16

    halo = lax.ppermute(frames[0, 2 * RD - 1 :], "rows", [(i, i + 1) for i in range(count - 1)])
    target_row, target_col, wv, conv_bias, proj_weight = prepare(
        target_row, target_col, conv_weight, conv_bias.reshape(1, C1), proj_weight
    )
    own = [frames[1]]
    for bit in reversed(range(3, bits)):
        own = own + [swap(block, 1 << bit, count) for block in own]
    across = [swap(own[0], 4, count)]
    own[-1], target_row, target_col, wv, conv_bias, proj_weight = lax.optimization_barrier(
        (own[-1], target_row, target_col, wv, conv_bias, proj_weight)
    )
    across = across + [swap(block, 4, count) for block in own[1:]]
    own = jnp.concatenate(own, axis=0)
    own_far = swap(own, 2, count)
    across = jnp.concatenate(across, axis=0)
    target_row, target_col, cotangent, across = lax.optimization_barrier(
        (target_row, target_col, cotangent, across)
    )
    across_far = swap(across, 2, count)
    grad, grad_t = scatter(ny, target_row, target_col, cotangent)
    near = jnp.concatenate([own, across, own_far, across_far], axis=0)
    near, grad, halo = lax.optimization_barrier((near, grad, halo))
    far = swap(near, 1, count)
    kept, sent, sums_kept, sums_sent, hid, first, first_grad = main(
        count, bits, quarter, me_word, near, far, frames[0], halo, wv,
        conv_bias, proj_weight, grad, grad_t,
    )

    other_sums = swap(sums_sent, 1, count)
    other = swap(sent, 1, count)
    given_sums, sums = plus(sums_kept[1], other_sums[1]), plus(sums_kept[0], other_sums[0])
    given, pixels = plus(kept[1], other[1]), plus(kept[0], other[0])
    given_sums, given = lax.optimization_barrier((given_sums, given))
    sums = plus(sums, swap(given_sums, 2, count))
    pixels = plus(pixels, swap(given, 2, count))
    for bit in range(2, bits):
        sums = plus(sums, swap(sums, 1 << bit, count))
        if bit < bits - 1:
            sums, pixels, target_row = lax.optimization_barrier((sums, pixels, target_row))
        else:
            lookups = lookup(ny, target_row, target_col, hid, first, proj_weight)
            sums, pixels, lookups = lax.optimization_barrier((sums, pixels, lookups))
        half = pixels.shape[0] // 2
        pixels = plus(pixels[:half], swap(pixels[half:], 1 << bit, count))
    near = jnp.stack([sums, swap(sums, 2, count)])
    near, pixels = lax.optimization_barrier((near, pixels))
    far = swap(near, 1, count)
    grad_input = input_grad(first_grad, pixels, wv)
    grad_conv, grad_bias, grad_proj = final(quarter, me_word, near, far)
    return lookups, grad_input, grad_conv, grad_bias.reshape(C1), grad_proj


def solution(mesh):
    split = P(None, ("pairs", "rows"))
    return jax.shard_map(
        per_device,
        mesh=mesh,
        in_specs=(P(None, ("pairs", "rows"), None), P(), P(), P(), split, split, split),
        out_specs=(
            split,
            P(None, ("pairs", "rows"), None),
            P("pairs", None),
            P("pairs"),
            P("pairs", None),
        ),
        check_vma=False,
    )
```

```python
import functools

import jax
import jax.numpy as jnp
from jax import lax
from jax.experimental import pallas as pl
from jax.experimental.pallas import tpu as pltpu
from jax.sharding import PartitionSpec as P

C = 256
C1 = 128
C0 = 96
LEVELS = 4
SPAN = 9
ITERS = 12
RD = 8
WC = 16
LOOKS = 3888
PIX = RD * WC
WIN = 384
BLOCK = PIX + 2 * WC
CHUNKS = [slice(k * LOOKS // 3, (k + 1) * LOOKS // 3) for k in range(3)]
F32 = jnp.float32
BF16 = jnp.bfloat16


def vmem_of(ny):
    return pltpu.CompilerParams(vmem_limit_bytes=(8 + ny * 3 // 16) * 1024 * 1024)

def dot(a, b):
    return jnp.dot(a, b, preferred_element_type=F32)

def dot_nt(a, b):
    return lax.dot_general(a, b, (((1,), (1,)), ((), ())), preferred_element_type=F32)

def dot_tn(a, b):
    return lax.dot_general(a, b, (((0,), (0,)), ((), ())), preferred_element_type=F32)

def iota(shape, dim):
    return lax.broadcasted_iota(jnp.int32, shape, dim)

def pick(tile, index):
    return jnp.take_along_axis(tile, index, axis=0, mode="promise_in_bounds")

def pool_matrix(ny):
    parts = []
    for level in range(1, LEVELS):
        shape = (ny >> level, ny)
        hit = iota(shape, 0) == (iota(shape, 1) >> level)
        parts.append(jnp.where(hit, 0.25**level, 0.0))
    return jnp.concatenate(parts, axis=0).astype(BF16)

def spread_matrix(ny):
    parts = []
    for level in range(1, LEVELS):
        shape = (ny, ny >> level)
        hit = (iota(shape, 0) >> level) == iota(shape, 1)
        parts.append(jnp.where(hit, 0.25**level, 0.0))
    return jnp.concatenate(parts, axis=1).astype(BF16)

def identity():
    return jnp.where(iota((C1, C1), 0) == iota((C1, C1), 1), 1.0, 0.0).astype(BF16)


def lane_row(ref, step):
    return jnp.broadcast_to(ref[pl.ds(step, 1), :], (8, PIX))

def place_columns(source, offset, cols):
    values = list(source)
    bit = 1
    while bit < cols:
        taken = (offset & bit) != 0
        last = 2 * bit >= cols
        size = len(values)
        moved = []
        for k in range(size + bit):
            if last and not 4 <= k < cols + 4:
                moved.append(None)
                continue
            here = values[k] if k < size else None
            back = values[k - bit] if 0 <= k - bit < size else None
            here = jnp.zeros((8, PIX), F32) if here is None else here
            back = jnp.zeros((8, PIX), F32) if back is None else back
            moved.append(jnp.where(taken, back, here))
        values = moved
        bit *= 2
    return values[4 : cols + 4]

def window_columns(source, offset, cols):
    zero = jnp.zeros((8, PIX), F32)
    values = [zero] * 4 + list(source) + [zero] * 4
    bit = cols // 2
    while bit >= 1:
        taken = (offset & bit) != 0
        values = [jnp.where(taken, values[k + bit], values[k]) for k in range(bit + 8)]
        bit //= 2
    return values

def scatter_kernel(
    ny, row_ref, col_ref, cot_hbm, grad_ref, grad_t_ref, cot_in, cot, packed, sems, *sums
):
    sub = iota((8, PIX), 0)
    loads = [
        pltpu.make_async_copy(cot_hbm.at[part], cot_in.at[part], sems.at[k])
        for k, part in enumerate(CHUNKS)
    ]
    for load in loads:
        load.start()
    for level in range(LEVELS):
        sums[level][...] = jnp.zeros(sums[level].shape, F32)
    def step(t, carry):
        row_all, col_all = lane_row(row_ref, t), lane_row(col_ref, t)
        for level in range(LEVELS):
            cols, tiles = WC >> level, ny >> (level + 3)
            base = t * 324 + level * 81
            start = (row_all >> level) + 4
            col = col_all >> level
            shift, tile_at = start & 7, start >> 3
            body = [cot[pl.ds(base + dx, 8, stride=SPAN), :] for dx in range(SPAN)]
            tail = [
                jnp.broadcast_to(cot[pl.ds(base + 72 + dx, 1), :], (8, PIX)) for dx in range(SPAN)
            ]
            body = place_columns(body, col, cols)
            tail = place_columns(tail, col, cols)
            index = (sub - shift) & 7
            upper, lower, edge = sub >= shift, sub < shift, sub == shift
            hits = [tile_at == k for k in range(tiles + 1)]
            for v in range(cols):
                turned = pick(body[v], index)
                high = jnp.where(upper, turned, 0.0)
                low = jnp.where(lower, turned, jnp.where(edge, tail[v], 0.0))
                for k in range(tiles):
                    term = jnp.where(hits[k + 1], high, jnp.where(hits[k], low, 0.0))
                    sums[level][v, 8 * k : 8 * k + 8, :] += term
        return carry

    for k, part in enumerate(CHUNKS):
        loads[k].wait()
        cot[part, :] = cot_in[part, :].astype(F32)
        lax.fori_loop(4 * k, 4 * k + 4, step, 0)
    at = 0
    for level in range(1, LEVELS):
        for pair in range(WC // 2):
            packed[at : at + (ny >> level), pair * PIX : pair * PIX + PIX] = sums[level][
                pair >> (level - 1)
            ].astype(BF16)
        at += ny >> level
    added = dot(spread_matrix(ny), packed[...])
    for v in range(WC):
        lanes = slice(v // 2 * PIX, v // 2 * PIX + PIX)
        grad_ref[v] = (sums[0][v] + added[:, lanes]).astype(BF16)
    grad_t_ref[...] = dot_nt(identity(), grad_ref[...].reshape(WC * ny, PIX)).astype(BF16)

def scatter(ny, target_row, target_col, cotangent):
    vmem = pl.BlockSpec(memory_space=pltpu.VMEM)
    return pl.pallas_call(
        functools.partial(scatter_kernel, ny),
        out_shape=(
            jax.ShapeDtypeStruct((WC, ny, PIX), BF16),
            jax.ShapeDtypeStruct((PIX, WC * ny), BF16),
        ),
        in_specs=[vmem, vmem, pl.BlockSpec(memory_space=pl.ANY)],
        scratch_shapes=[
            pltpu.VMEM((LOOKS, PIX), BF16),
            pltpu.VMEM((LOOKS, PIX), F32),
            pltpu.VMEM((ny * 7 // 8, WC // 2 * PIX), BF16),
            pltpu.SemaphoreType.DMA((3,)),
        ]
        + [pltpu.VMEM((WC >> level, ny >> level, PIX), F32) for level in range(LEVELS)],
        compiler_params=vmem_of(ny),
        cost_estimate=pl.CostEstimate(flops=10**9, bytes_accessed=4 * 10**6, transcendentals=0),
        name="scatter",
    )(target_row, target_col, cotangent)

def prepare_kernel(row_ref, col_ref, w_ref, bias_ref, proj_ref, row_out, col_out, wv_ref, bias_out, proj_out):
    row_out[...] = row_ref[...]
    col_out[...] = col_ref[...]
    bias_out[...] = bias_ref[...]
    proj_out[...] = proj_ref[...]
    wv_ref[...] = jnp.zeros(wv_ref.shape, BF16)
    for tap in range(3):
        lanes = slice(tap * C1, tap * C1 + C1)
        rows = w_ref[tap * 288 : tap * 288 + 288, :]
        wv_ref[0, 32:320, lanes] = rows
        wv_ref[1, 96:384, lanes] = rows


def prepare(target_row, target_col, conv_weight, conv_bias, proj_weight):
    same = [jax.ShapeDtypeStruct(a.shape, a.dtype) for a in (target_row, conv_bias, proj_weight)]
    return pl.pallas_call(
        prepare_kernel,
        out_shape=(
            same[0], same[0], jax.ShapeDtypeStruct((2, WIN, WIN), BF16), same[1], same[2]
        ),
        compiler_params=vmem_of(0),
        cost_estimate=pl.CostEstimate(flops=10**6, bytes_accessed=10**6, transcendentals=0),
        name="prepare",
    )(target_row, target_col, conv_weight, conv_bias, proj_weight)


def lookup_kernel(
    ny, row_ref, col_ref, hid_ref, first_ref, proj_ref, out_hbm, looked, out, second, wide, pooled,
    sems, *volumes
):
    sub = iota((8, PIX), 0)
    first = first_ref[...]
    zero = jnp.zeros((8, PIX), F32)
    for level in range(LEVELS):
        for v in range(WC >> level):
            volumes[level][v, 0:8, :] = zero
            volumes[level][v, 8 + (ny >> level) :, :] = zero
    second[...] = dot(hid_ref[...].reshape(WC * ny, C1), proj_ref[...]).astype(BF16)
    for v in range(WC):
        wide[:, v * C : v * C + C] = second[v * ny : v * ny + ny, :]
    means = dot(pool_matrix(ny), wide[...])
    at = done = 0
    for level in range(1, LEVELS):
        size = ny >> level
        for v in range(WC >> level):
            first_at = v << level
            total = means[done : done + size, first_at * C : first_at * C + C]
            for k in range(first_at + 1, first_at + (1 << level)):
                total = total + means[done : done + size, k * C : k * C + C]
            pooled[at : at + size, :] = total.astype(BF16)
            at += size
        done += size
    scores = dot_nt(second[...], first) * (1.0 / 16.0)
    for v in range(WC):
        volumes[0][v, 8 : 8 + ny, :] = scores[v * ny : v * ny + ny]
    scores = dot_nt(pooled[...], first) * (1.0 / 16.0)
    at = 0
    for level in range(1, LEVELS):
        size = ny >> level
        for v in range(WC >> level):
            volumes[level][v, 8 : 8 + size, :] = scores[at : at + size]
            at += size

    def step(t, carry):
        row_all, col_all = lane_row(row_ref, t), lane_row(col_ref, t)
        for level in range(LEVELS):
            cols, tiles = WC >> level, ny >> (level + 3)
            base = t * 324 + level * 81
            start = (row_all >> level) + 4
            col = col_all >> level
            shift, tile_at = start & 7, start >> 3
            index = (sub + shift) & 7
            upper = sub >= shift
            beyond = tile_at >= tiles
            body, tail = [], []
            for v in range(cols):
                held = [volumes[level][v, 8 * k : 8 * k + 8, :] for k in range(tiles + 2)]
                for k in range(2):
                    held[k] = jnp.where(beyond, held[tiles + k], held[k])
                bit = tiles // 2
                while bit >= 1:
                    taken = (tile_at & bit) != 0
                    held = [jnp.where(taken, held[k + bit], held[k]) for k in range(bit + 1)]
                    bit //= 2
                body.append(pick(jnp.where(upper, held[0], held[1]), index))
                tail.append(pick(held[1], shift))
            body = window_columns(body, col, cols)
            tail = window_columns(tail, col, cols)
            for dx in range(SPAN):
                looked[pl.ds(base + dx, 8, stride=SPAN), :] = body[dx]
                looked[pl.ds(base + 72 + dx, 1), :] = tail[dx][0:1]
        return carry

    stores = []
    for k, part in enumerate(CHUNKS):
        lax.fori_loop(4 * k, 4 * k + 4, step, 0)
        out[part, :] = looked[part, :].astype(BF16)
        stores.append(pltpu.make_async_copy(out.at[part], out_hbm.at[part], sems.at[k]))
        stores[k].start()
    for store in stores:
        store.wait()

def lookup(ny, target_row, target_col, hid, first, proj_weight):
    return pl.pallas_call(
        functools.partial(lookup_kernel, ny),
        out_shape=jax.ShapeDtypeStruct((LOOKS, PIX), BF16),
        out_specs=pl.BlockSpec(memory_space=pl.ANY),
        scratch_shapes=[
            pltpu.VMEM((LOOKS, PIX), F32),
            pltpu.VMEM((LOOKS, PIX), BF16),
            pltpu.VMEM((WC * ny, C), BF16),
            pltpu.VMEM((ny, WC * C), BF16),
            pltpu.VMEM((ny * 21 // 4, C), BF16),
            pltpu.SemaphoreType.DMA((3,)),
        ]
        + [pltpu.VMEM((WC >> level, (ny >> level) + 16, PIX), F32) for level in range(LEVELS)],
        compiler_params=vmem_of(ny),
        cost_estimate=pl.CostEstimate(flops=10**9, bytes_accessed=4 * 10**6, transcendentals=0),
        name="lookup",
    )(target_row, target_col, hid, first, proj_weight)


def reverse_bits(value, bits):
    total = 0
    for bit in range(bits):
        total = total | (((value >> bit) & 1) << (bits - 1 - bit))
    return total


def row_pick(me, count, bits):
    shape = (3 * count * RD, 2 * count * RD)
    row, at = iota(shape, 0), iota(shape, 1)
    kind, row = row // (count * RD), row % (count * RD)
    line = 2 * row + jnp.where(kind == 2, -1, kind)
    place = reverse_bits(((line >> 4) & (count - 1)) ^ me, bits) * (2 * RD) + (line & 15)
    return jnp.where((place == at) & (line >= 0), 1.0, 0.0).astype(BF16)


def own_pick():
    shape = (6 * RD, 2 * RD)
    row, at = iota(shape, 0), iota(shape, 1)
    kind, row = row >> 4, row & 15
    line = 2 * row + jnp.where(kind == 2, -1, kind)
    return jnp.where((line == at) & (row < RD), 1.0, 0.0).astype(BF16)


def pixel_pick(transposed):
    a, b = iota((PIX, PIX), 0), iota((PIX, PIX), 1)
    a, b = (b, a) if transposed else (a, b)
    return jnp.where(a == (b & 7) * WC + (b >> 3), 1.0, 0.0).astype(BF16)


def main_kernel(
    count, bits, quarter, me_ref, maps0_ref, maps1_ref, maps2_ref, maps3_ref, own_ref, halo_ref, wv_ref, bias_ref, proj_ref,
    grad_ref, grad_t_ref, kept_ref, sent_ref, sums_kept_ref, sums_sent_ref, hid_ref, first_ref,
    first_grad_ref, views, inner, grads, rows_out, turned, pre0, below, wsum
):
    ny = count * RD
    span = 8 * ny
    me = me_ref[0]

    def place_rows(start, step, lanes_of):
        for q in range(8):
            rows = slice(start + step * q, start + step * q + step)
            after = slice(start + step * (q + 1), start + step * (q + 2))
            value = lanes_of(slice(q * WIN, q * WIN + WIN))
            for kind in range(3):
                part = value[step * kind : step * kind + step]
                views[kind, 1, rows, :] = part
                views[kind, 0, rows, 128:WIN] = part[:, 0:256]
                if q == 0:
                    views[kind, 0, rows, 0:128] = jnp.zeros((step, 128), BF16)
                if q < 7:
                    views[kind, 0, after, 0:128] = part[:, 256:WIN]

    picks = row_pick(me, count, bits)
    own_picks = own_pick()
    at_halo = iota((6 * RD, WIN), 0) == 4 * RD

    def owned(lanes):
        top = jnp.broadcast_to(halo_ref[:, lanes].astype(F32), (6 * RD, WIN))
        return jnp.where(at_halo, top, dot(own_picks, own_ref[:, lanes])).astype(BF16)

    place_rows(span, 2 * RD, owned)

    def gathered(lanes):
        refs = (maps0_ref, maps1_ref, maps2_ref, maps3_ref)
        rows = jnp.concatenate([ref[:, lanes] for ref in refs], axis=0)
        return dot(picks, rows).astype(BF16)

    place_rows(0, ny, gathered)

    bias = bias_ref[...]
    for g in range(2):
        inner[...] = (
            dot(views[0, g], wv_ref[g, :, C1 : 2 * C1])
            + dot(views[1, g], wv_ref[g, :, 2 * C1 : 3 * C1])
            + dot(views[2, g], wv_ref[g, :, 0:C1])
            + bias
        )
        for q in range(8):
            c = 2 * q + g
            hid_ref[c] = jnp.maximum(inner[q * ny : q * ny + ny, :], 0.0).astype(BF16)
            row = span + 2 * RD * q
            pre0[8 * c : 8 * c + 8, :] = inner[row : row + 8, :]

    proj = proj_ref[...]
    hid0 = dot(pixel_pick(False), jnp.maximum(pre0[...], 0.0).astype(BF16)).astype(BF16)
    first = dot(hid0, proj).astype(BF16)
    first_ref[...] = first
    fold = (dot_nt(first, proj) * (1.0 / 16.0)).astype(BF16)
    mixed = (dot(grad_t_ref[...], hid_ref[...].reshape(WC * ny, C1)) * (1.0 / 16.0)).astype(BF16)
    grad_first = dot(mixed, proj).astype(BF16)
    grad_proj = dot_tn(mixed, first) + dot_tn(hid0, grad_first)
    pre_grad0 = dot(pixel_pick(True), dot_nt(grad_first, proj).astype(BF16))
    pre_grad0 = jnp.where(pre0[...] > 0.0, pre_grad0, 0.0)
    first_grad_ref[...] = pre_grad0.astype(BF16)
    pre0[...] = pre_grad0

    one = identity()
    bias_sum = jnp.sum(pre_grad0, axis=0, keepdims=True)
    zeros8 = jnp.zeros((8, C1), F32)
    all_grads = dot(grad_ref[...].reshape(WC * ny, PIX), fold)
    for g in range(2):
        for q in range(8):
            c = 2 * q + g
            grad = jnp.where(hid_ref[c].astype(F32) > 0.0, all_grads[c * ny : c * ny + ny], 0.0)
            bias_sum = bias_sum + jnp.sum(grad, axis=0, keepdims=True)
            grads[c, 0:ny, :] = grad
            grads[c, ny : ny + 8, :] = zeros8
            rows_out[g, q * ny : q * ny + ny, :] = grad.astype(BF16)
            own_grad = jnp.concatenate([pre_grad0[8 * c : 8 * c + 8], zeros8], axis=0)
            row = span + 2 * RD * q
            rows_out[g, row : row + 2 * RD, :] = own_grad.astype(BF16)
        turned[g] = dot_nt(one, rows_out[g]).astype(BF16)

    first_tops = pre0[pl.ds(0, WC, stride=RD), :]
    for place in range(count):
        device = reverse_bits(place, bits) ^ me
        row = pl.multiple_of(device * RD, RD)
        dest = (kept_ref, sent_ref)[place // (count // 2)]
        group = place // (count // 4) % 2
        at = BLOCK * (place % (count // 4))
        for c in range(0, WC, 2):
            dest[group, at + RD * c : at + RD * c + 2 * RD, :] = jnp.concatenate(
                [grads[c, pl.ds(row, RD), :], grads[c + 1, pl.ds(row, RD), :]], axis=0
            ).astype(BF16)
        for c in range(WC):
            below[c : c + 1, :] = grads[c, pl.ds(row + RD, 1), :]
        dest[group, at + PIX : at + PIX + WC, :] = below[...].astype(BF16)
        dest[group, at + PIX + WC : at + BLOCK, :] = jnp.where(
            device + 1 == me, first_tops, 0.0
        ).astype(BF16)

    parts = [[dot(turned[g], views[kind, g]) for g in range(2)] for kind in range(3)]
    wsum[9 * C0 + 2 * C1 :, :] = jnp.zeros((4 * quarter - 9 * C0 - 2 * C1, C1), F32)
    for tap in range(3):
        left, right = parts[(tap - 1) % 3]
        wsum[tap * 288 : tap * 288 + 288, :] = left.T[32:320] + right.T[96:384]
    wsum[9 * C0 : 9 * C0 + C1, :] = grad_proj[:, 0:C1]
    wsum[9 * C0 + C1 : 9 * C0 + 2 * C1, :] = grad_proj[:, C1:]
    wsum[9 * C0 + 2 * C1 : 9 * C0 + 2 * C1 + 1, :] = bias_sum
    for place in range(4):
        row = pl.multiple_of((place ^ reverse_bits(me & 3, 2)) * quarter, 16)
        dest = (sums_kept_ref, sums_sent_ref)[place // 2]
        dest[place % 2] = wsum[pl.ds(row, quarter), :].astype(BF16)


def main(count, bits, quarter, me, maps, own, halo, wv, bias, proj_weight, grad, grad_t):
    ny = count * RD
    rows = 8 * ny + PIX
    vmem = pl.BlockSpec(memory_space=pltpu.VMEM)
    pixels, sums = (2, BLOCK * count // 4, C1), (2, quarter, C1)
    return pl.pallas_call(
        functools.partial(main_kernel, count, bits, quarter),
        in_specs=[pl.BlockSpec(memory_space=pltpu.SMEM)] + [vmem] * 11,
        out_shape=(
            jax.ShapeDtypeStruct(pixels, BF16),
            jax.ShapeDtypeStruct(pixels, BF16),
            jax.ShapeDtypeStruct(sums, BF16),
            jax.ShapeDtypeStruct(sums, BF16),
            jax.ShapeDtypeStruct((WC, ny, C1), BF16),
            jax.ShapeDtypeStruct((PIX, C), BF16),
            jax.ShapeDtypeStruct((PIX, C1), BF16),
        ),
        scratch_shapes=[
            pltpu.VMEM((3, 2, rows, WIN), BF16),
            pltpu.VMEM((rows, C1), F32),
            pltpu.VMEM((WC, ny + 8, C1), F32),
            pltpu.VMEM((2, rows, C1), BF16),
            pltpu.VMEM((2, C1, rows), BF16),
            pltpu.VMEM((PIX, C1), F32),
            pltpu.VMEM((WC, C1), F32),
            pltpu.VMEM((4 * quarter, C1), F32),
        ],
        compiler_params=vmem_of(ny),
        cost_estimate=pl.CostEstimate(flops=4 * 10**9, bytes_accessed=6 * 10**6, transcendentals=0),
        name="features",
    )(me, *maps, own, halo, wv, bias, proj_weight, grad, grad_t)


def input_kernel(first_ref, block_ref, wv_ref, out_ref, sides, full):
    last = iota((8, C1), 0) == 7
    grads = [first_ref[...].astype(F32), block_ref[0:PIX, :].astype(F32)]
    border = block_ref[PIX:, :].astype(F32)

    def spread(g):
        here, both = [], []
        for c in range(g, WC, 2):
            for f in range(2):
                own = grads[f][8 * c : 8 * c + 8]
                at = WC * (1 - f) + c
                below = jnp.broadcast_to(border[at : at + 1], (8, C1))
                here.append(own)
                both.append(
                    jnp.concatenate([own, jnp.where(last, below, pltpu.roll(own, 7, 0))], axis=1)
                )
        here = jnp.concatenate(here, axis=0).astype(BF16)
        both = jnp.concatenate(both, axis=0).astype(BF16)
        weights = wv_ref[g]
        outer = jnp.concatenate([weights[:, 2 * C1 : 3 * C1], weights[:, 0:C1]], axis=1)
        return dot_nt(here, weights[:, C1 : 2 * C1]), dot_nt(both, outer)

    even, odd = spread(0), spread(1)
    for parity in range(2):
        for q in range(8):
            sides[parity, :, q * WIN : q * WIN + WIN] = odd[parity][16 * q : 16 * q + 16]
        sides[parity, :, 0:256] += even[parity][0:16, 128:WIN]
        for q in range(1, 8):
            sides[parity, :, q * WIN - 128 : q * WIN + 256] += even[parity][16 * q : 16 * q + 16]
        for f in range(2):
            for j in range(2 * WC * C0 // 128):
                lanes = slice(128 * j, 128 * j + 128)
                full[f, j, pl.ds(parity, 8, stride=2), :] = sides[parity, 8 * f : 8 * f + 8, lanes]
    for f in range(2):
        for j in range(2 * WC * C0 // 128):
            out_ref[f, :, 128 * j : 128 * j + 128] = full[f, j].astype(BF16)


def input_grad(first_grad, block, wv):
    return pl.pallas_call(
        input_kernel,
        out_shape=jax.ShapeDtypeStruct((2, 2 * RD, 2 * WC * C0), BF16),
        scratch_shapes=[
            pltpu.VMEM((2, 2 * RD, 2 * WC * C0), F32),
            pltpu.VMEM((2, 2 * WC * C0 // 128, 2 * RD, 128), F32),
        ],
        compiler_params=vmem_of(0),
        cost_estimate=pl.CostEstimate(flops=10**8, bytes_accessed=10**6, transcendentals=0),
        name="input_grad",
    )(first_grad, block, wv)


def final_kernel(quarter, me_ref, near_ref, far_ref, conv_ref, bias_ref, proj_ref, wsum):
    turned = reverse_bits(me_ref[0] & 3, 2)
    for place in range(4):
        ref = (near_ref, far_ref)[place // 2]
        row = pl.multiple_of((place ^ turned) * quarter, 16)
        wsum[pl.ds(row, quarter), :] = ref[place % 2].astype(F32)
    conv_ref[...] = wsum[0 : 9 * C0, :]
    proj_ref[:, 0:C1] = wsum[9 * C0 : 9 * C0 + C1, :]
    proj_ref[:, C1:] = wsum[9 * C0 + C1 : 9 * C0 + 2 * C1, :]
    bias_ref[...] = wsum[9 * C0 + 2 * C1 : 9 * C0 + 2 * C1 + 1, :]


def final(quarter, me, near, far):
    vmem = pl.BlockSpec(memory_space=pltpu.VMEM)
    return pl.pallas_call(
        functools.partial(final_kernel, quarter),
        in_specs=[pl.BlockSpec(memory_space=pltpu.SMEM), vmem, vmem],
        out_shape=(
            jax.ShapeDtypeStruct((9 * C0, C1), F32),
            jax.ShapeDtypeStruct((1, C1), F32),
            jax.ShapeDtypeStruct((C1, C), F32),
        ),
        scratch_shapes=[pltpu.VMEM((4 * quarter, C1), F32)],
        compiler_params=vmem_of(0),
        name="weight_grads",
    )(me, near, far)


def swap(value, bit, count):
    return lax.ppermute(value, "rows", [(i, i ^ bit) for i in range(count)])


def plus(a, b):
    return (a.astype(F32) + b.astype(F32)).astype(BF16)


def per_device(frames, conv_weight, conv_bias, proj_weight, target_row, target_col, cotangent):
    count = lax.axis_size("rows")
    bits = count.bit_length() - 1
    ny = count * RD
    me_word = lax.axis_index("rows").astype(jnp.int32).reshape(1)
    quarter = -(-(9 * C0 + 2 * C1 + 1) // 64) * 16

    halo = lax.ppermute(frames[0, 2 * RD - 1 :], "rows", [(i, i + 1) for i in range(count - 1)])
    target_row, target_col, wv, conv_bias, proj_weight = prepare(
        target_row, target_col, conv_weight, conv_bias.reshape(1, C1), proj_weight
    )
    own = [frames[1]]
    for bit in reversed(range(3, bits)):
        own = own + [swap(block, 1 << bit, count) for block in own]
    across = [swap(own[0], 4, count)]
    own[-1], target_row, target_col, wv, conv_bias, proj_weight = lax.optimization_barrier(
        (own[-1], target_row, target_col, wv, conv_bias, proj_weight)
    )
    across = across + [swap(block, 4, count) for block in own[1:]]
    own = jnp.concatenate(own, axis=0)
    own_far = swap(own, 2, count)
    across = jnp.concatenate(across, axis=0)
    target_row, target_col, cotangent, across = lax.optimization_barrier(
        (target_row, target_col, cotangent, across)
    )
    across_far = swap(across, 2, count)
    grad, grad_t = scatter(ny, target_row, target_col, cotangent)
    near = jnp.concatenate([own, across], axis=0)
    other = swap(near, 1, count)
    far = jnp.concatenate([own_far, across_far], axis=0)
    far, grad, halo, other = lax.optimization_barrier((far, grad, halo, other))
    maps = near, far, other, swap(far, 1, count)
    kept, sent, sums_kept, sums_sent, hid, first, first_grad = main(
        count, bits, quarter, me_word, maps, frames[0], halo, wv,
        conv_bias, proj_weight, grad, grad_t,
    )

    other_sums = swap(sums_sent, 1, count)
    other = swap(sent, 1, count)
    given_sums, sums = plus(sums_kept[1], other_sums[1]), plus(sums_kept[0], other_sums[0])
    given, pixels = plus(kept[1], other[1]), plus(kept[0], other[0])
    given_sums, given = lax.optimization_barrier((given_sums, given))
    sums = plus(sums, swap(given_sums, 2, count))
    pixels = plus(pixels, swap(given, 2, count))
    for bit in range(2, bits):
        sums = plus(sums, swap(sums, 1 << bit, count))
        if bit < bits - 1:
            sums, pixels, target_row = lax.optimization_barrier((sums, pixels, target_row))
        else:
            lookups = lookup(ny, target_row, target_col, hid, first, proj_weight)
            sums, pixels, lookups = lax.optimization_barrier((sums, pixels, lookups))
        half = pixels.shape[0] // 2
        pixels = plus(pixels[:half], swap(pixels[half:], 1 << bit, count))
    near = jnp.stack([sums, swap(sums, 2, count)])
    near, pixels = lax.optimization_barrier((near, pixels))
    far = swap(near, 1, count)
    grad_input = input_grad(first_grad, pixels, wv)
    grad_conv, grad_bias, grad_proj = final(quarter, me_word, near, far)
    return lookups, grad_input, grad_conv, grad_bias.reshape(C1), grad_proj


def solution(mesh):
    split = P(None, ("pairs", "rows"))
    return jax.shard_map(
        per_device,
        mesh=mesh,
        in_specs=(P(None, ("pairs", "rows"), None), P(), P(), P(), split, split, split),
        out_specs=(
            split,
            P(None, ("pairs", "rows"), None),
            P("pairs", None),
            P("pairs"),
            P("pairs", None),
        ),
        check_vma=False,
    )
```

```python
import functools

import jax
import jax.numpy as jnp
from jax import lax
from jax.experimental import pallas as pl
from jax.experimental.pallas import tpu as pltpu
from jax.sharding import PartitionSpec as P

C = 256
C1 = 128
C0 = 96
LEVELS = 4
SPAN = 9
ITERS = 12
RD = 8
WC = 16
LOOKS = 3888
PIX = RD * WC
WIN = 384
BLOCK = PIX + 2 * WC
CHUNKS = [slice(k * LOOKS // 3, (k + 1) * LOOKS // 3) for k in range(3)]
F32 = jnp.float32
BF16 = jnp.bfloat16


def vmem_of(ny):
    return pltpu.CompilerParams(vmem_limit_bytes=(8 + ny * 3 // 16) * 1024 * 1024)

def dot(a, b):
    return jnp.dot(a, b, preferred_element_type=F32)

def dot_nt(a, b):
    return lax.dot_general(a, b, (((1,), (1,)), ((), ())), preferred_element_type=F32)

def dot_tn(a, b):
    return lax.dot_general(a, b, (((0,), (0,)), ((), ())), preferred_element_type=F32)

def iota(shape, dim):
    return lax.broadcasted_iota(jnp.int32, shape, dim)

def pick(tile, index):
    return jnp.take_along_axis(tile, index, axis=0, mode="promise_in_bounds")

def pool_matrix(ny):
    parts = []
    for level in range(1, LEVELS):
        shape = (ny >> level, ny)
        hit = iota(shape, 0) == (iota(shape, 1) >> level)
        parts.append(jnp.where(hit, 0.25**level, 0.0))
    return jnp.concatenate(parts, axis=0).astype(BF16)

def spread_matrix(ny):
    parts = []
    for level in range(1, LEVELS):
        shape = (ny, ny >> level)
        hit = (iota(shape, 0) >> level) == iota(shape, 1)
        parts.append(jnp.where(hit, 0.25**level, 0.0))
    return jnp.concatenate(parts, axis=1).astype(BF16)

def identity():
    return jnp.where(iota((C1, C1), 0) == iota((C1, C1), 1), 1.0, 0.0).astype(BF16)


def lane_row(ref, step):
    return jnp.broadcast_to(ref[pl.ds(step, 1), :], (8, PIX))

def place_columns(source, offset, cols):
    values = list(source)
    bit = 1
    while bit < cols:
        taken = (offset & bit) != 0
        last = 2 * bit >= cols
        size = len(values)
        moved = []
        for k in range(size + bit):
            if last and not 4 <= k < cols + 4:
                moved.append(None)
                continue
            here = values[k] if k < size else None
            back = values[k - bit] if 0 <= k - bit < size else None
            here = jnp.zeros((8, PIX), F32) if here is None else here
            back = jnp.zeros((8, PIX), F32) if back is None else back
            moved.append(jnp.where(taken, back, here))
        values = moved
        bit *= 2
    return values[4 : cols + 4]

def window_columns(source, offset, cols):
    zero = jnp.zeros((8, PIX), F32)
    values = [zero] * 4 + list(source) + [zero] * 4
    bit = cols // 2
    while bit >= 1:
        taken = (offset & bit) != 0
        values = [jnp.where(taken, values[k + bit], values[k]) for k in range(bit + 8)]
        bit //= 2
    return values

def scatter_kernel(
    ny, row_ref, col_ref, cot_hbm, grad_ref, grad_t_ref, cot_in, cot, packed, sems, *sums
):
    sub = iota((8, PIX), 0)
    loads = [
        pltpu.make_async_copy(cot_hbm.at[part], cot_in.at[part], sems.at[k])
        for k, part in enumerate(CHUNKS)
    ]
    for load in loads:
        load.start()
    for level in range(LEVELS):
        sums[level][...] = jnp.zeros(sums[level].shape, F32)
    def step(t, carry):
        row_all, col_all = lane_row(row_ref, t), lane_row(col_ref, t)
        for level in range(LEVELS):
            cols, tiles = WC >> level, ny >> (level + 3)
            base = t * 324 + level * 81
            start = (row_all >> level) + 4
            col = col_all >> level
            shift, tile_at = start & 7, start >> 3
            body = [cot[pl.ds(base + dx, 8, stride=SPAN), :] for dx in range(SPAN)]
            tail = [
                jnp.broadcast_to(cot[pl.ds(base + 72 + dx, 1), :], (8, PIX)) for dx in range(SPAN)
            ]
            body = place_columns(body, col, cols)
            tail = place_columns(tail, col, cols)
            index = (sub - shift) & 7
            upper, lower, edge = sub >= shift, sub < shift, sub == shift
            hits = [tile_at == k for k in range(tiles + 1)]
            for v in range(cols):
                turned = pick(body[v], index)
                high = jnp.where(upper, turned, 0.0)
                low = jnp.where(lower, turned, jnp.where(edge, tail[v], 0.0))
                for k in range(tiles):
                    term = jnp.where(hits[k + 1], high, jnp.where(hits[k], low, 0.0))
                    sums[level][v, 8 * k : 8 * k + 8, :] += term
        return carry

    for k, part in enumerate(CHUNKS):
        loads[k].wait()
        cot[part, :] = cot_in[part, :].astype(F32)
        lax.fori_loop(4 * k, 4 * k + 4, step, 0)
    at = 0
    for level in range(1, LEVELS):
        for pair in range(WC // 2):
            packed[at : at + (ny >> level), pair * PIX : pair * PIX + PIX] = sums[level][
                pair >> (level - 1)
            ].astype(BF16)
        at += ny >> level
    added = dot(spread_matrix(ny), packed[...])
    for v in range(WC):
        lanes = slice(v // 2 * PIX, v // 2 * PIX + PIX)
        grad_ref[v] = (sums[0][v] + added[:, lanes]).astype(BF16)
    grad_t_ref[...] = dot_nt(identity(), grad_ref[...].reshape(WC * ny, PIX)).astype(BF16)

def scatter(ny, target_row, target_col, cotangent):
    vmem = pl.BlockSpec(memory_space=pltpu.VMEM)
    return pl.pallas_call(
        functools.partial(scatter_kernel, ny),
        out_shape=(
            jax.ShapeDtypeStruct((WC, ny, PIX), BF16),
            jax.ShapeDtypeStruct((PIX, WC * ny), BF16),
        ),
        in_specs=[vmem, vmem, pl.BlockSpec(memory_space=pl.ANY)],
        scratch_shapes=[
            pltpu.VMEM((LOOKS, PIX), BF16),
            pltpu.VMEM((LOOKS, PIX), F32),
            pltpu.VMEM((ny * 7 // 8, WC // 2 * PIX), BF16),
            pltpu.SemaphoreType.DMA((3,)),
        ]
        + [pltpu.VMEM((WC >> level, ny >> level, PIX), F32) for level in range(LEVELS)],
        compiler_params=vmem_of(ny),
        cost_estimate=pl.CostEstimate(flops=10**9, bytes_accessed=4 * 10**6, transcendentals=0),
        name="scatter",
    )(target_row, target_col, cotangent)

def prepare_kernel(row_ref, col_ref, w_ref, bias_ref, proj_ref, row_out, col_out, wv_ref, bias_out, proj_out):
    row_out[...] = row_ref[...]
    col_out[...] = col_ref[...]
    bias_out[...] = bias_ref[...]
    proj_out[...] = proj_ref[...]
    wv_ref[...] = jnp.zeros(wv_ref.shape, BF16)
    for tap in range(3):
        at = (tap - 1) % 3 * WIN
        rows = w_ref[tap * 288 : tap * 288 + 288, :]
        wv_ref[0, at + 32 : at + 320, :] = rows
        wv_ref[1, at + 96 : at + 384, :] = rows


def prepare(target_row, target_col, conv_weight, conv_bias, proj_weight):
    same = [jax.ShapeDtypeStruct(a.shape, a.dtype) for a in (target_row, conv_bias, proj_weight)]
    return pl.pallas_call(
        prepare_kernel,
        out_shape=(
            same[0], same[0], jax.ShapeDtypeStruct((2, 3 * WIN, C1), BF16), same[1], same[2]
        ),
        compiler_params=vmem_of(0),
        cost_estimate=pl.CostEstimate(flops=10**6, bytes_accessed=10**6, transcendentals=0),
        name="prepare",
    )(target_row, target_col, conv_weight, conv_bias, proj_weight)


def lookup_kernel(
    ny, row_ref, col_ref, hid_ref, first_ref, proj_ref, out_hbm, looked, out, second, wide, pooled,
    sems, *volumes
):
    sub = iota((8, PIX), 0)
    first = first_ref[...]
    zero = jnp.zeros((8, PIX), F32)
    for level in range(LEVELS):
        for v in range(WC >> level):
            volumes[level][v, 0:8, :] = zero
            volumes[level][v, 8 + (ny >> level) :, :] = zero
    second[...] = dot(hid_ref[...].reshape(WC * ny, C1), proj_ref[...]).astype(BF16)
    for v in range(WC):
        wide[:, v * C : v * C + C] = second[v * ny : v * ny + ny, :]
    means = dot(pool_matrix(ny), wide[...])
    at = done = 0
    for level in range(1, LEVELS):
        size = ny >> level
        for v in range(WC >> level):
            first_at = v << level
            total = means[done : done + size, first_at * C : first_at * C + C]
            for k in range(first_at + 1, first_at + (1 << level)):
                total = total + means[done : done + size, k * C : k * C + C]
            pooled[at : at + size, :] = total.astype(BF16)
            at += size
        done += size
    scores = dot_nt(second[...], first) * (1.0 / 16.0)
    for v in range(WC):
        volumes[0][v, 8 : 8 + ny, :] = scores[v * ny : v * ny + ny]
    scores = dot_nt(pooled[...], first) * (1.0 / 16.0)
    at = 0
    for level in range(1, LEVELS):
        size = ny >> level
        for v in range(WC >> level):
            volumes[level][v, 8 : 8 + size, :] = scores[at : at + size]
            at += size

    def step(t, carry):
        row_all, col_all = lane_row(row_ref, t), lane_row(col_ref, t)
        for level in range(LEVELS):
            cols, tiles = WC >> level, ny >> (level + 3)
            base = t * 324 + level * 81
            start = (row_all >> level) + 4
            col = col_all >> level
            shift, tile_at = start & 7, start >> 3
            index = (sub + shift) & 7
            upper = sub >= shift
            beyond = tile_at >= tiles
            body, tail = [], []
            for v in range(cols):
                held = [volumes[level][v, 8 * k : 8 * k + 8, :] for k in range(tiles + 2)]
                for k in range(2):
                    held[k] = jnp.where(beyond, held[tiles + k], held[k])
                bit = tiles // 2
                while bit >= 1:
                    taken = (tile_at & bit) != 0
                    held = [jnp.where(taken, held[k + bit], held[k]) for k in range(bit + 1)]
                    bit //= 2
                body.append(pick(jnp.where(upper, held[0], held[1]), index))
                tail.append(pick(held[1], shift))
            body = window_columns(body, col, cols)
            tail = window_columns(tail, col, cols)
            for dx in range(SPAN):
                looked[pl.ds(base + dx, 8, stride=SPAN), :] = body[dx]
                looked[pl.ds(base + 72 + dx, 1), :] = tail[dx][0:1]
        return carry

    stores = []
    for k, part in enumerate(CHUNKS):
        lax.fori_loop(4 * k, 4 * k + 4, step, 0)
        out[part, :] = looked[part, :].astype(BF16)
        stores.append(pltpu.make_async_copy(out.at[part], out_hbm.at[part], sems.at[k]))
        stores[k].start()
    for store in stores:
        store.wait()

def lookup(ny, target_row, target_col, hid, first, proj_weight):
    return pl.pallas_call(
        functools.partial(lookup_kernel, ny),
        out_shape=jax.ShapeDtypeStruct((LOOKS, PIX), BF16),
        out_specs=pl.BlockSpec(memory_space=pl.ANY),
        scratch_shapes=[
            pltpu.VMEM((LOOKS, PIX), F32),
            pltpu.VMEM((LOOKS, PIX), BF16),
            pltpu.VMEM((WC * ny, C), BF16),
            pltpu.VMEM((ny, WC * C), BF16),
            pltpu.VMEM((ny * 21 // 4, C), BF16),
            pltpu.SemaphoreType.DMA((3,)),
        ]
        + [pltpu.VMEM((WC >> level, (ny >> level) + 16, PIX), F32) for level in range(LEVELS)],
        compiler_params=vmem_of(ny),
        cost_estimate=pl.CostEstimate(flops=10**9, bytes_accessed=4 * 10**6, transcendentals=0),
        name="lookup",
    )(target_row, target_col, hid, first, proj_weight)


def reverse_bits(value, bits):
    total = 0
    for bit in range(bits):
        total = total | (((value >> bit) & 1) << (bits - 1 - bit))
    return total


def row_pick(me, count, bits):
    shape = (3 * count * RD, 2 * count * RD)
    row, at = iota(shape, 0), iota(shape, 1)
    kind, row = row // (count * RD), row % (count * RD)
    line = 2 * row + jnp.where(kind == 2, -1, kind)
    place = reverse_bits(((line >> 4) & (count - 1)) ^ me, bits) * (2 * RD) + (line & 15)
    return jnp.where((place == at) & (line >= 0), 1.0, 0.0).astype(BF16)


def own_pick():
    shape = (6 * RD, 2 * RD)
    row, at = iota(shape, 0), iota(shape, 1)
    kind, row = row >> 4, row & 15
    line = 2 * row + jnp.where(kind == 2, -1, kind)
    return jnp.where((line == at) & (row < RD), 1.0, 0.0).astype(BF16)


def pixel_pick(transposed):
    a, b = iota((PIX, PIX), 0), iota((PIX, PIX), 1)
    a, b = (b, a) if transposed else (a, b)
    return jnp.where(a == (b & 7) * WC + (b >> 3), 1.0, 0.0).astype(BF16)


def main_kernel(
    count, bits, quarter, me_ref, maps0_ref, maps1_ref, maps2_ref, maps3_ref, own_ref, halo_ref, wv_ref, bias_ref, proj_ref,
    grad_ref, grad_t_ref, kept_ref, sent_ref, sums_kept_ref, sums_sent_ref, hid_ref, first_ref,
    first_grad_ref, views, inner, grads, rows_out, turned, pre0, below, wsum
):
    ny = count * RD
    span = 8 * ny
    me = me_ref[0]

    def place_rows(start, step, lanes_of):
        for q in range(8):
            rows = slice(start + step * q, start + step * q + step)
            after = slice(start + step * (q + 1), start + step * (q + 2))
            value = lanes_of(slice(q * WIN, q * WIN + WIN))
            for kind in range(3):
                part = value[step * kind : step * kind + step]
                lane = kind * WIN
                views[1, rows, lane : lane + WIN] = part
                views[0, rows, lane + 128 : lane + WIN] = part[:, 0:256]
                if q == 0:
                    views[0, rows, lane : lane + 128] = jnp.zeros((step, 128), BF16)
                if q < 7:
                    views[0, after, lane : lane + 128] = part[:, 256:WIN]

    picks = row_pick(me, count, bits)
    own_picks = own_pick()
    at_halo = iota((6 * RD, WIN), 0) == 4 * RD

    def owned(lanes):
        top = jnp.broadcast_to(halo_ref[:, lanes].astype(F32), (6 * RD, WIN))
        return jnp.where(at_halo, top, dot(own_picks, own_ref[:, lanes])).astype(BF16)

    place_rows(span, 2 * RD, owned)

    def gathered(lanes):
        refs = (maps0_ref, maps1_ref, maps2_ref, maps3_ref)
        rows = jnp.concatenate([ref[:, lanes] for ref in refs], axis=0)
        return dot(picks, rows).astype(BF16)

    place_rows(0, ny, gathered)

    bias = bias_ref[...]
    for g in range(2):
        inner[...] = dot(views[g], wv_ref[g]) + bias
        for q in range(8):
            c = 2 * q + g
            hid_ref[c] = jnp.maximum(inner[q * ny : q * ny + ny, :], 0.0).astype(BF16)
            row = span + 2 * RD * q
            pre0[8 * c : 8 * c + 8, :] = inner[row : row + 8, :]

    proj = proj_ref[...]
    hid0 = dot(pixel_pick(False), jnp.maximum(pre0[...], 0.0).astype(BF16)).astype(BF16)
    first = dot(hid0, proj).astype(BF16)
    first_ref[...] = first
    fold = (dot_nt(first, proj) * (1.0 / 16.0)).astype(BF16)
    mixed = (dot(grad_t_ref[...], hid_ref[...].reshape(WC * ny, C1)) * (1.0 / 16.0)).astype(BF16)
    grad_first = dot(mixed, proj).astype(BF16)
    grad_proj = dot_tn(mixed, first) + dot_tn(hid0, grad_first)
    pre_grad0 = dot(pixel_pick(True), dot_nt(grad_first, proj).astype(BF16))
    pre_grad0 = jnp.where(pre0[...] > 0.0, pre_grad0, 0.0)
    first_grad_ref[...] = pre_grad0.astype(BF16)
    pre0[...] = pre_grad0

    one = identity()
    bias_sum = jnp.sum(pre_grad0, axis=0, keepdims=True)
    zeros8 = jnp.zeros((8, C1), F32)
    all_grads = dot(grad_ref[...].reshape(WC * ny, PIX), fold)
    for g in range(2):
        for q in range(8):
            c = 2 * q + g
            grad = jnp.where(hid_ref[c].astype(F32) > 0.0, all_grads[c * ny : c * ny + ny], 0.0)
            bias_sum = bias_sum + jnp.sum(grad, axis=0, keepdims=True)
            grads[c, 0:ny, :] = grad
            grads[c, ny : ny + 8, :] = zeros8
            rows_out[g, q * ny : q * ny + ny, :] = grad.astype(BF16)
            own_grad = jnp.concatenate([pre_grad0[8 * c : 8 * c + 8], zeros8], axis=0)
            row = span + 2 * RD * q
            rows_out[g, row : row + 2 * RD, :] = own_grad.astype(BF16)
        turned[g] = dot_nt(one, rows_out[g]).astype(BF16)

    first_tops = pre0[pl.ds(0, WC, stride=RD), :]
    for place in range(count):
        device = reverse_bits(place, bits) ^ me
        row = pl.multiple_of(device * RD, RD)
        dest = (kept_ref, sent_ref)[place // (count // 2)]
        group = place // (count // 4) % 2
        at = BLOCK * (place % (count // 4))
        for c in range(0, WC, 2):
            dest[group, at + RD * c : at + RD * c + 2 * RD, :] = jnp.concatenate(
                [grads[c, pl.ds(row, RD), :], grads[c + 1, pl.ds(row, RD), :]], axis=0
            ).astype(BF16)
        for c in range(WC):
            below[c : c + 1, :] = grads[c, pl.ds(row + RD, 1), :]
        dest[group, at + PIX : at + PIX + WC, :] = below[...].astype(BF16)
        dest[group, at + PIX + WC : at + BLOCK, :] = jnp.where(
            device + 1 == me, first_tops, 0.0
        ).astype(BF16)

    parts = [dot(turned[g], views[g]) for g in range(2)]
    wsum[9 * C0 + 2 * C1 :, :] = jnp.zeros((4 * quarter - 9 * C0 - 2 * C1, C1), F32)
    for tap in range(3):
        lanes = slice((tap - 1) % 3 * WIN, (tap - 1) % 3 * WIN + WIN)
        left, right = parts[0][:, lanes], parts[1][:, lanes]
        wsum[tap * 288 : tap * 288 + 288, :] = left.T[32:320] + right.T[96:384]
    wsum[9 * C0 : 9 * C0 + C1, :] = grad_proj[:, 0:C1]
    wsum[9 * C0 + C1 : 9 * C0 + 2 * C1, :] = grad_proj[:, C1:]
    wsum[9 * C0 + 2 * C1 : 9 * C0 + 2 * C1 + 1, :] = bias_sum
    for place in range(4):
        row = pl.multiple_of((place ^ reverse_bits(me & 3, 2)) * quarter, 16)
        dest = (sums_kept_ref, sums_sent_ref)[place // 2]
        dest[place % 2] = wsum[pl.ds(row, quarter), :].astype(BF16)


def main(count, bits, quarter, me, maps, own, halo, wv, bias, proj_weight, grad, grad_t):
    ny = count * RD
    rows = 8 * ny + PIX
    vmem = pl.BlockSpec(memory_space=pltpu.VMEM)
    pixels, sums = (2, BLOCK * count // 4, C1), (2, quarter, C1)
    return pl.pallas_call(
        functools.partial(main_kernel, count, bits, quarter),
        in_specs=[pl.BlockSpec(memory_space=pltpu.SMEM)] + [vmem] * 11,
        out_shape=(
            jax.ShapeDtypeStruct(pixels, BF16),
            jax.ShapeDtypeStruct(pixels, BF16),
            jax.ShapeDtypeStruct(sums, BF16),
            jax.ShapeDtypeStruct(sums, BF16),
            jax.ShapeDtypeStruct((WC, ny, C1), BF16),
            jax.ShapeDtypeStruct((PIX, C), BF16),
            jax.ShapeDtypeStruct((PIX, C1), BF16),
        ),
        scratch_shapes=[
            pltpu.VMEM((2, rows, 3 * WIN), BF16),
            pltpu.VMEM((rows, C1), F32),
            pltpu.VMEM((WC, ny + 8, C1), F32),
            pltpu.VMEM((2, rows, C1), BF16),
            pltpu.VMEM((2, C1, rows), BF16),
            pltpu.VMEM((PIX, C1), F32),
            pltpu.VMEM((WC, C1), F32),
            pltpu.VMEM((4 * quarter, C1), F32),
        ],
        compiler_params=vmem_of(ny),
        cost_estimate=pl.CostEstimate(flops=4 * 10**9, bytes_accessed=6 * 10**6, transcendentals=0),
        name="features",
    )(me, *maps, own, halo, wv, bias, proj_weight, grad, grad_t)


def input_kernel(first_ref, block_ref, wv_ref, out_ref, sides, full):
    last = iota((8, C1), 0) == 7
    grads = [first_ref[...].astype(F32), block_ref[0:PIX, :].astype(F32)]
    border = block_ref[PIX:, :].astype(F32)

    def spread(g):
        here, both = [], []
        for c in range(g, WC, 2):
            for f in range(2):
                own = grads[f][8 * c : 8 * c + 8]
                at = WC * (1 - f) + c
                below = jnp.broadcast_to(border[at : at + 1], (8, C1))
                here.append(own)
                both.append(
                    jnp.concatenate([own, jnp.where(last, below, pltpu.roll(own, 7, 0))], axis=1)
                )
        here = jnp.concatenate(here, axis=0).astype(BF16)
        both = jnp.concatenate(both, axis=0).astype(BF16)
        weights = wv_ref[g]
        outer = jnp.concatenate([weights[WIN : 2 * WIN], weights[2 * WIN :]], axis=1)
        return dot_nt(here, weights[0:WIN]), dot_nt(both, outer)

    even, odd = spread(0), spread(1)
    for parity in range(2):
        for q in range(8):
            sides[parity, :, q * WIN : q * WIN + WIN] = odd[parity][16 * q : 16 * q + 16]
        sides[parity, :, 0:256] += even[parity][0:16, 128:WIN]
        for q in range(1, 8):
            sides[parity, :, q * WIN - 128 : q * WIN + 256] += even[parity][16 * q : 16 * q + 16]
        for f in range(2):
            for j in range(2 * WC * C0 // 128):
                lanes = slice(128 * j, 128 * j + 128)
                full[f, j, pl.ds(parity, 8, stride=2), :] = sides[parity, 8 * f : 8 * f + 8, lanes]
    for f in range(2):
        for j in range(2 * WC * C0 // 128):
            out_ref[f, :, 128 * j : 128 * j + 128] = full[f, j].astype(BF16)


def input_grad(first_grad, block, wv):
    return pl.pallas_call(
        input_kernel,
        out_shape=jax.ShapeDtypeStruct((2, 2 * RD, 2 * WC * C0), BF16),
        scratch_shapes=[
            pltpu.VMEM((2, 2 * RD, 2 * WC * C0), F32),
            pltpu.VMEM((2, 2 * WC * C0 // 128, 2 * RD, 128), F32),
        ],
        compiler_params=vmem_of(0),
        cost_estimate=pl.CostEstimate(flops=10**8, bytes_accessed=10**6, transcendentals=0),
        name="input_grad",
    )(first_grad, block, wv)


def final_kernel(quarter, me_ref, near_ref, far_ref, conv_ref, bias_ref, proj_ref, wsum):
    turned = reverse_bits(me_ref[0] & 3, 2)
    for place in range(4):
        ref = (near_ref, far_ref)[place // 2]
        row = pl.multiple_of((place ^ turned) * quarter, 16)
        wsum[pl.ds(row, quarter), :] = ref[place % 2].astype(F32)
    conv_ref[...] = wsum[0 : 9 * C0, :]
    proj_ref[:, 0:C1] = wsum[9 * C0 : 9 * C0 + C1, :]
    proj_ref[:, C1:] = wsum[9 * C0 + C1 : 9 * C0 + 2 * C1, :]
    bias_ref[...] = wsum[9 * C0 + 2 * C1 : 9 * C0 + 2 * C1 + 1, :]


def final(quarter, me, near, far):
    vmem = pl.BlockSpec(memory_space=pltpu.VMEM)
    return pl.pallas_call(
        functools.partial(final_kernel, quarter),
        in_specs=[pl.BlockSpec(memory_space=pltpu.SMEM), vmem, vmem],
        out_shape=(
            jax.ShapeDtypeStruct((9 * C0, C1), F32),
            jax.ShapeDtypeStruct((1, C1), F32),
            jax.ShapeDtypeStruct((C1, C), F32),
        ),
        scratch_shapes=[pltpu.VMEM((4 * quarter, C1), F32)],
        compiler_params=vmem_of(0),
        name="weight_grads",
    )(me, near, far)


def swap(value, bit, count):
    return lax.ppermute(value, "rows", [(i, i ^ bit) for i in range(count)])


def plus(a, b):
    return (a.astype(F32) + b.astype(F32)).astype(BF16)


def per_device(frames, conv_weight, conv_bias, proj_weight, target_row, target_col, cotangent):
    count = lax.axis_size("rows")
    bits = count.bit_length() - 1
    ny = count * RD
    me_word = lax.axis_index("rows").astype(jnp.int32).reshape(1)
    quarter = -(-(9 * C0 + 2 * C1 + 1) // 64) * 16

    halo = lax.ppermute(frames[0, 2 * RD - 1 :], "rows", [(i, i + 1) for i in range(count - 1)])
    target_row, target_col, wv, conv_bias, proj_weight = prepare(
        target_row, target_col, conv_weight, conv_bias.reshape(1, C1), proj_weight
    )
    own = [frames[1]]
    for bit in reversed(range(3, bits)):
        own = own + [swap(block, 1 << bit, count) for block in own]
    across = [swap(own[0], 4, count)]
    own[-1], target_row, target_col, wv, conv_bias, proj_weight = lax.optimization_barrier(
        (own[-1], target_row, target_col, wv, conv_bias, proj_weight)
    )
    across = across + [swap(block, 4, count) for block in own[1:]]
    own = jnp.concatenate(own, axis=0)
    own_far = swap(own, 2, count)
    across = jnp.concatenate(across, axis=0)
    target_row, target_col, cotangent, across = lax.optimization_barrier(
        (target_row, target_col, cotangent, across)
    )
    across_far = swap(across, 2, count)
    grad, grad_t = scatter(ny, target_row, target_col, cotangent)
    near = jnp.concatenate([own, across], axis=0)
    other = swap(near, 1, count)
    far = jnp.concatenate([own_far, across_far], axis=0)
    far, grad, halo, other = lax.optimization_barrier((far, grad, halo, other))
    maps = near, far, other, swap(far, 1, count)
    kept, sent, sums_kept, sums_sent, hid, first, first_grad = main(
        count, bits, quarter, me_word, maps, frames[0], halo, wv,
        conv_bias, proj_weight, grad, grad_t,
    )

    other_sums = swap(sums_sent, 1, count)
    other = swap(sent, 1, count)
    given_sums, sums = plus(sums_kept[1], other_sums[1]), plus(sums_kept[0], other_sums[0])
    given, pixels = plus(kept[1], other[1]), plus(kept[0], other[0])
    given_sums, given = lax.optimization_barrier((given_sums, given))
    sums = plus(sums, swap(given_sums, 2, count))
    lookups = lookup(ny, target_row, target_col, hid, first, proj_weight)
    sums, lookups = lax.optimization_barrier((sums, lookups))
    pixels = plus(pixels, swap(given, 2, count))
    for bit in range(2, bits):
        sums = plus(sums, swap(sums, 1 << bit, count))
        sums, pixels = lax.optimization_barrier((sums, pixels))
        half = pixels.shape[0] // 2
        pixels = plus(pixels[:half], swap(pixels[half:], 1 << bit, count))
    near = jnp.stack([sums, swap(sums, 2, count)])
    near, pixels = lax.optimization_barrier((near, pixels))
    far = swap(near, 1, count)
    grad_input = input_grad(first_grad, pixels, wv)
    grad_conv, grad_bias, grad_proj = final(quarter, me_word, near, far)
    return lookups, grad_input, grad_conv, grad_bias.reshape(C1), grad_proj


def solution(mesh):
    split = P(None, ("pairs", "rows"))
    return jax.shard_map(
        per_device,
        mesh=mesh,
        in_specs=(P(None, ("pairs", "rows"), None), P(), P(), P(), split, split, split),
        out_specs=(
            split,
            P(None, ("pairs", "rows"), None),
            P("pairs", None),
            P("pairs"),
            P("pairs", None),
        ),
        check_vma=False,
    )
```
